128 devices in a mesh: freq: 16 (over z, y_hi, core), blk: 8 (over y_lo, x).
Axes of the slice: x: 4, y: 4 (y_hi: 2, y_lo: 2; y = y_hi * 2 + y_lo), z: 4, core: 2. Of those that a mesh axis runs over, the one named last changes fastest.
Arguments:
- voltages: bfloat16 [2, 2048, 126976], P(None, ('freq', 'blk')), may hold values from -6 to 6
- pfb_taps: float32 [16, 4096], replicated, may hold values from -1.5 to 1.5
- order_table: int32 [8, 256], P('blk'), may hold values from 0 to 255, as said below
- lag_table: int32 [4], replicated, may hold values from 0 to 3, each once
Outputs:
- visibility: bfloat16 [128, 8, 4, 2, 256, 256], P('freq', 'blk')
- far_visibility: bfloat16 [64, 8, 2, 256, 256], P('freq', 'blk')
The draws below stay inside these ranges and needn't reach their ends.
Inputs may be any that keep to these rules, and one draw needn't show every extreme that they name: Each row of order_table holds every number below 256 once. lag_table holds every number below 4 once.
All inputs are finite; a program needn't handle non-finite values.
Results may differ from the reference program's by a relative error of at most 0.007.
Values may be sent and summed in bfloat16 or wider, within the bound.
A program may use at most 192 MiB of HBM per device.

```python
import math
import jax
import jax.numpy as jnp
from jax import lax

CH = 4096
TAPS = 16
AVG = 32
SPECTRA = 16
BLOCKS = 8
LAGS = 4
BI = 256
INPUTS = 2048
NSAMP = 126976
NOUT = 128


def draw_order_table(key, part):
    key = jax.random.fold_in(key, 7)
    block_keys = jax.random.split(key, BLOCKS)
    return jax.vmap(lambda block_key: jax.random.permutation(block_key, BI))(block_keys).astype(jnp.int32)


def block_levels(stream_key, shape, cuts, least, high):
    def one(dim, blocks):
        draws = jax.random.uniform(jax.random.fold_in(jax.random.fold_in(stream_key, 6), dim), (blocks,), jnp.float32, least / len(cuts), high / len(cuts))
        return jnp.repeat(jnp.exp(draws), shape[dim] // blocks).reshape((-1,) + (1,) * (len(shape) - dim - 1))

    level = one(*cuts[0])
    for cut in cuts[1:]:
        level = level * one(*cut)
    return level


def normal_values(rng, dims, deviation, bound, cuts=(), kind=jnp.bfloat16):
    entries = jax.random.normal(rng, dims, jnp.float32) * deviation
    if len(cuts) > 0:
        entries = block_levels(rng, dims, cuts, -0.22, 0.18) * entries
    return jnp.clip(entries, min=-bound, max=bound).astype(kind)


def setup_inputs(seed: int = 0) -> dict:
    splits = jax.random.split(jax.random.key(seed), 5)
    return {
        "voltages": normal_values(splits[0], (2, INPUTS, NSAMP), 1.0, 6.0, ((1, 128),)),
        "pfb_taps": normal_values(splits[1], (TAPS, CH), 0.25, 1.5, (), jnp.float32),
        "order_table": draw_order_table(jax.random.fold_in(splits[4], 71), 0),
        "lag_table": jax.random.permutation(splits[3], LAGS).astype(jnp.int32),
    }


def filter_bank(samples, pfb_taps):
    inputs = samples.shape[1]
    framed = samples.astype(jnp.float32).reshape(2, inputs, SPECTRA + TAPS - 1, CH)
    filtered = jnp.zeros((2, inputs, SPECTRA, CH), jnp.float32)
    for tap_index in range(TAPS):
        filtered = filtered + pfb_taps[tap_index] * framed[:, :, tap_index:tap_index + SPECTRA]
    rounded = filtered.astype(jnp.bfloat16).astype(jnp.float32)
    spectrum = jnp.fft.fft(lax.complex(rounded[0], rounded[1]), axis=-1) * (1.0 / math.sqrt(CH))
    pieces = jnp.stack([jnp.real(spectrum), jnp.imag(spectrum)]).astype(jnp.bfloat16)
    pieces = pieces.reshape(2, inputs, SPECTRA, NOUT, AVG).transpose(0, 1, 3, 4, 2)
    return pieces.reshape(2, inputs, NOUT, AVG * SPECTRA)

def correlate(left_side, right_side):
    left_wide = left_side.astype(jnp.float32)
    right_wide = right_side.astype(jnp.float32)
    real_part = jnp.einsum('prok,pcok->orc', left_wide, right_wide)
    imag_part = jnp.einsum('rok,cok->orc', left_wide[1], right_wide[0]) - jnp.einsum('rok,cok->orc', left_wide[0], right_wide[1])
    return jnp.stack([real_part, imag_part], axis=1) * (1.0 / (AVG * SPECTRA))

def take_parity(array, parity, axis):
    shape = array.shape
    split = shape[:axis] + (shape[axis] // 2, 2) + shape[axis + 1:]
    return lax.dynamic_index_in_dim(array.reshape(split), parity, axis + 1, keepdims=False)

def reference(voltages, pfb_taps, order_table, lag_table):
    grouped = voltages.reshape(2, BI, BLOCKS, NSAMP)

    def one_block(position):
        samples = lax.dynamic_index_in_dim(grouped, position, 2, keepdims=False)
        pieces = filter_bank(samples, pfb_taps)
        row_order = lax.dynamic_index_in_dim(order_table, position, 0, keepdims=False)
        return jnp.take(pieces, row_order.astype(jnp.int32), axis=1)
    spectra = lax.map(one_block, jnp.arange(BLOCKS, dtype=jnp.int32))

    def pair_tiles(position):
        own_block = spectra[position]
        near_tiles = []
        for slot_index in range(LAGS):
            partner = ((position + lag_table[slot_index]) % BLOCKS).astype(jnp.int32)
            near_tiles.append(correlate(own_block, spectra[partner]).astype(jnp.bfloat16))
        far_partner = ((position + LAGS) % BLOCKS).astype(jnp.int32)
        parity = (position >= LAGS).astype(jnp.int32)
        own_half = take_parity(own_block, parity, 2)
        far_half = take_parity(spectra[far_partner], parity, 2)
        return (jnp.stack(near_tiles, axis=1), correlate(own_half, far_half).astype(jnp.bfloat16))
    near_part, far_part = lax.map(pair_tiles, jnp.arange(BLOCKS, dtype=jnp.int32))
    return (near_part.transpose(1, 0, 2, 3, 4, 5), far_part.transpose(1, 0, 2, 3, 4))
```

```python
import functools
import math

import jax
import jax.numpy as jnp
import numpy as np
from jax import lax
from jax.experimental import pallas as pl
from jax.experimental.pallas import tpu as pltpu
from jax.sharding import PartitionSpec as P

CH = 4096
TAPS = 16
SPECTRA = 16
COLS = 32
LANES = 128
GROUP = 4
GROUPS = 4


def complex_mul(value, turn):
    real, imag = value
    cos, sin = float(turn.real), float(turn.imag)
    if abs(sin) < 1e-12 and abs(cos - 1) < 1e-12:
        return value
    if abs(cos) < 1e-12 and abs(sin + 1) < 1e-12:
        return (imag, -real)
    if abs(cos + sin) < 1e-12:
        return ((real + imag) * cos, (imag - real) * cos)
    if abs(cos - sin) < 1e-12:
        return ((real - imag) * cos, (real + imag) * cos)
    return (real * cos - imag * sin, real * sin + imag * cos)


def fft_list(values):
    count = len(values)
    if count == 1:
        return values
    if count == 2:
        (ar, ai), (br, bi) = values
        return [(ar + br, ai + bi), (ar - br, ai - bi)]
    if count == 4:
        even = fft_list([values[0], values[2]])
        odd = fft_list([values[1], values[3]])
    else:
        even = fft_list(values[0::2])
        odd = fft_list(values[1::2])
    half = count // 2
    low, high = [], []
    for index in range(half):
        turned = complex_mul(odd[index], np.exp(-2j * np.pi * index / count))
        base = even[index]
        low.append((base[0] + turned[0], base[1] + turned[1]))
        high.append((base[0] - turned[0], base[1] - turned[1]))
    return low + high


def fft_columns(values):
    sections = []
    for low in range(8):
        parts = fft_list([values[8 * high + low] for high in range(4)])
        sections.append([complex_mul(part, np.exp(-2j * np.pi * low * index / 32)) for index, part in enumerate(parts)])
    result = [None] * 32
    for index in range(4):
        parts = fft_list([sections[low][index] for low in range(8)])
        for high in range(8):
            result[index + 4 * high] = parts[high]
    return result


def channelize_kernel(volt, taps, turn_cos, turn_sin, dft_high, dft_low, out, filt, z_real, z_imag, wide):
    group = pl.program_id(0)

    def filter_column(col, carry):
        weights = [jnp.broadcast_to(taps[pl.ds(t, 1), pl.ds(pl.multiple_of(col * LANES, LANES), LANES)], (16, LANES)) for t in range(TAPS)]
        for part in range(2):
            frames = []
            for frame in range(GROUP + TAPS - 1):
                start = pl.multiple_of((group * GROUP + frame) * CH + col * LANES, LANES)
                frames.append(volt[part, :, pl.ds(start, LANES)].astype(jnp.float32))
            for spec in range(GROUP):
                total = weights[0] * frames[spec]
                for tap in range(1, TAPS):
                    total = total + weights[tap] * frames[spec + tap]
                filt[part, spec, col] = total.astype(jnp.bfloat16)
        return carry

    lax.fori_loop(0, COLS, filter_column, 0)

    for spec in range(GROUP):
        for half in range(2):
            rows = slice(half * 8, half * 8 + 8)
            values = []
            for col in range(COLS):
                values.append(tuple(filt[part, spec, col].astype(jnp.float32)[rows] for part in range(2)))
            for index, (real, imag) in enumerate(fft_columns(values)):
                cos, sin = turn_cos[index], turn_sin[index]
                place = pl.ds(half * LANES + spec * COLS + index, 8, stride=2 * LANES)
                z_real[place, :] = real * cos - imag * sin
                z_imag[place, :] = real * sin + imag * cos

    def last_step(block, carry):
        rows = pl.ds(pl.multiple_of(block * 256, 256), 256)
        both = jnp.concatenate([z_real[rows, :], z_imag[rows, :]], axis=1)
        high = both.astype(jnp.bfloat16)
        low = (both - high.astype(jnp.float32)).astype(jnp.bfloat16)
        dims = (((1,), (1,)), ((), ()))
        total = lax.dot_general(dft_high[...], high, dims, preferred_element_type=jnp.float32)
        total = total + lax.dot_general(dft_low[...], high, dims, preferred_element_type=jnp.float32)
        total = total + lax.dot_general(dft_high[...], low, dims, preferred_element_type=jnp.float32)
        for part in range(2):
            for half in range(2):
                piece = total[part * 128:part * 128 + 128, half * 128:half * 128 + 128]
                wide[pl.ds(block * 4 + part * 2 + half, 128, stride=32), :] = piece
        return carry

    lax.fori_loop(0, 8, last_step, 0)

    def narrow(index, carry):
        rows = pl.ds(pl.multiple_of(index * 256, 256), 256)
        out[pl.ds(index * 8, 8), 0] = wide[rows, :].astype(jnp.bfloat16).reshape(8, 32, LANES)
        return carry

    lax.fori_loop(0, 16, narrow, 0)


def tables():
    rows = np.arange(COLS)[:, None] * np.arange(LANES)[None, :]
    angles = -2.0 * np.pi * rows / CH
    cos = np.repeat(np.cos(angles)[:, None, :], 8, 1) / 64
    sin = np.repeat(np.sin(angles)[:, None, :], 8, 1) / 64
    steps = np.arange(LANES)
    turn = -2.0 * np.pi * (steps[:, None] * steps[None, :] % LANES) / LANES
    dft = np.block([[np.cos(turn), -np.sin(turn)], [np.sin(turn), np.cos(turn)]]).astype(np.float32)
    high = jnp.asarray(dft).astype(jnp.bfloat16)
    low = (jnp.asarray(dft) - high.astype(jnp.float32)).astype(jnp.bfloat16)
    return jnp.asarray(cos, jnp.float32), jnp.asarray(sin, jnp.float32), high, low


def whole(shape):
    return pl.BlockSpec(shape, lambda *_: (0,) * len(shape))


def channelize(voltages, pfb_taps):
    cos, sin, high, low = tables()
    inputs = [voltages, pfb_taps, cos, sin, high, low]
    return pl.pallas_call(
        channelize_kernel,
        grid=(GROUPS,),
        out_shape=jax.ShapeDtypeStruct((128, GROUPS, 32, LANES), jnp.bfloat16),
        in_specs=[whole(value.shape) for value in inputs],
        out_specs=pl.BlockSpec((128, 1, 32, LANES), lambda group: (0, group, 0, 0)),
        scratch_shapes=[
            pltpu.VMEM((2, GROUP, COLS, 16, LANES), jnp.bfloat16),
            pltpu.VMEM((2048, LANES), jnp.float32),
            pltpu.VMEM((2048, LANES), jnp.float32),
            pltpu.VMEM((4096, LANES), jnp.float32),
        ],
        compiler_params=pltpu.CompilerParams(vmem_limit_bytes=56 * 2**20),
    )(*inputs)


def correlate_kernel(lag_table, arrived, order, spread, near, far, natural, rows_x, rows_y):
    block = pl.program_id(0)
    dims = (((1,), (1,)), ((), ()))

    @pl.when(block == 0)
    def _():
        def unshuffle(index, carry):
            source = pl.ds(pl.multiple_of(index * 8, 8), 8)
            for pair in range(2):
                lanes = jnp.concatenate([arrived[source, 2 * pair + step].reshape(256, LANES) for step in range(2)], axis=1)
                sorted_rows = jnp.dot(spread[...], lanes, preferred_element_type=jnp.float32).astype(jnp.bfloat16)
                for member in range(8):
                    for part in range(2):
                        start = member * 32 + part * 16
                        natural[member, pl.ds(pl.multiple_of(index * 16, 16), 16), part * 512 + pair * 256:part * 512 + pair * 256 + 256] = sorted_rows[start:start + 16]
            return carry

        lax.fori_loop(0, 16, unshuffle, 0)
        members = lax.broadcasted_iota(jnp.int32, (256, 256), 1)
        for member in range(8):
            chosen = (order[:, member:member + 1] == members).astype(jnp.bfloat16)
            picked = jnp.dot(chosen, natural[member], preferred_element_type=jnp.float32)
            rows_x[member] = picked.astype(jnp.bfloat16)
            rows_y[member, :, :512] = picked[:, 512:].astype(jnp.bfloat16)
            rows_y[member, :, 512:] = (-picked[:, :512]).astype(jnp.bfloat16)

    def tiles(other, store):
        right = rows_x[other]
        for part, left in enumerate((rows_x, rows_y)):
            value = lax.dot_general(left[block], right, dims, preferred_element_type=jnp.float32)
            store(part, (value * (1.0 / 512)).astype(jnp.bfloat16))

    for slot in range(4):
        def store_near(part, value, slot=slot):
            near[0, slot, part] = value

        tiles(lax.rem(block + lag_table[slot], 8), store_near)

    def store_far(part, value):
        far[0, part] = value

    tiles(lax.rem(block + 4, 8), store_far)


def spread_table():
    table = np.zeros((256, 256), np.float32)
    for source in range(8):
        for row in range(16):
            for half in range(2):
                table[row * 16 + source * 2 + half, source * 32 + row * 2 + half] = 1
    return jnp.asarray(table).astype(jnp.bfloat16)


def correlate(arrived, order, lag_table):
    inputs = [arrived, order, spread_table()]
    return pl.pallas_call(
        correlate_kernel,
        grid=(8,),
        out_shape=(
            jax.ShapeDtypeStruct((8, 4, 2, 256, 256), jnp.bfloat16),
            jax.ShapeDtypeStruct((8, 2, 256, 256), jnp.bfloat16),
        ),
        in_specs=[pl.BlockSpec(memory_space=pltpu.SMEM)] + [whole(value.shape) for value in inputs],
        out_specs=(
            pl.BlockSpec((1, 4, 2, 256, 256), lambda block: (block, 0, 0, 0, 0)),
            pl.BlockSpec((1, 2, 256, 256), lambda block: (block, 0, 0, 0)),
        ),
        scratch_shapes=[pltpu.VMEM((8, 256, 1024), jnp.bfloat16)] * 3,
        compiler_params=pltpu.CompilerParams(vmem_limit_bytes=56 * 2**20),
    )(lag_table, *inputs)


def per_device(voltages, pfb_taps, order_table, lag_table):
    orders = lax.all_gather(order_table, "blk", axis=0, tiled=True)
    pieces = channelize(voltages, pfb_taps)
    arrived = lax.all_to_all(pieces, ("freq", "blk"), 0, 0, tiled=True)
    near, far = correlate(arrived, orders.T, lag_table)
    visibility = lax.all_to_all(near, "blk", 0, 0, tiled=True)
    far_all = lax.all_to_all(far, "blk", 0, 0, tiled=True)
    parity = (lax.axis_index("blk") >= 4).astype(jnp.int32)
    far_own = lax.dynamic_index_in_dim(far_all.reshape(4, 2, 2, 256, 256), parity, 1, keepdims=False)
    return visibility[:, None], far_own[:, None]


def solution(mesh):
    placed = (P(None, ("freq", "blk"), None), P(), P("blk", None), P())
    return jax.shard_map(
        per_device,
        mesh=mesh,
        in_specs=placed,
        out_specs=(P("freq", "blk", None, None, None, None), P("freq", "blk", None, None, None)),
        check_vma=False,
    )
```

```python
import functools
import math

import jax
import jax.numpy as jnp
import numpy as np
from jax import lax
from jax.experimental import pallas as pl
from jax.experimental.pallas import tpu as pltpu
from jax.sharding import PartitionSpec as P

CH = 4096
TAPS = 16
SPECTRA = 16
COLS = 32
LANES = 128
GROUP = 4
GROUPS = 4


def complex_mul(value, turn):
    real, imag = value
    cos, sin = float(turn.real), float(turn.imag)
    if abs(sin) < 1e-12 and abs(cos - 1) < 1e-12:
        return value
    if abs(cos) < 1e-12 and abs(sin + 1) < 1e-12:
        return (imag, -real)
    if abs(cos + sin) < 1e-12:
        return ((real + imag) * cos, (imag - real) * cos)
    if abs(cos - sin) < 1e-12:
        return ((real - imag) * cos, (real + imag) * cos)
    return (real * cos - imag * sin, real * sin + imag * cos)


def fft_list(values):
    count = len(values)
    if count == 1:
        return values
    if count == 2:
        (ar, ai), (br, bi) = values
        return [(ar + br, ai + bi), (ar - br, ai - bi)]
    if count == 4:
        even = fft_list([values[0], values[2]])
        odd = fft_list([values[1], values[3]])
    else:
        even = fft_list(values[0::2])
        odd = fft_list(values[1::2])
    half = count // 2
    low, high = [], []
    for index in range(half):
        turned = complex_mul(odd[index], np.exp(-2j * np.pi * index / count))
        base = even[index]
        low.append((base[0] + turned[0], base[1] + turned[1]))
        high.append((base[0] - turned[0], base[1] - turned[1]))
    return low + high


def fft_columns(values):
    sections = []
    for low in range(8):
        parts = fft_list([values[8 * high + low] for high in range(4)])
        sections.append([complex_mul(part, np.exp(-2j * np.pi * low * index / 32)) for index, part in enumerate(parts)])
    result = [None] * 32
    for index in range(4):
        parts = fft_list([sections[low][index] for low in range(8)])
        for high in range(8):
            result[index + 4 * high] = parts[high]
    return result


MESH = pl.DeviceIdType.MESH


def position():
    freq = lax.axis_index("freq")
    blk = lax.axis_index("blk")
    return (lax.rem(blk, 4), lax.rem(freq // 2, 2) * 2 + blk // 4, freq // 4, lax.rem(freq, 2))


def mesh_ids(col, row, layer, core):
    return (layer * 4 + (row // 2) * 2 + core, lax.rem(row, 2) * 4 + col)


def channelize_kernel(volt_far, taps, turn_cos, turn_sin, dft_high, dft_low, out, volt, filt, z_real, z_imag, wide, pieces, load_sem, send_sem, recv_sem, own_sem):
    def load(group):
        first = 0 if isinstance(group, int) and group == 0 else pl.multiple_of((group * GROUP + TAPS - 1) * CH, LANES)
        size = (GROUP + TAPS - 1) * CH if isinstance(group, int) and group == 0 else GROUP * CH
        place = (slice(None), slice(None), pl.ds(first, size))
        return pltpu.make_async_copy(volt_far.at[place], volt.at[place], load_sem.at[group])

    load(0).start()
    for later in range(1, GROUPS):
        load(jnp.int32(later)).start()

    col, row, layer, core = position()
    own_freq, own_blk = mesh_ids(col, row, layer, core)
    me = own_freq * 8 + own_blk

    def target(index):
        step = lax.rem(index * 75, 128)
        return mesh_ids(
            lax.rem(col + lax.rem(step, 4), 4),
            lax.rem(row + lax.rem(step // 4, 4), 4),
            lax.rem(layer + lax.rem(step // 16, 4), 4),
            lax.rem(core + step // 64, 2),
        )

    barrier = pltpu.get_barrier_semaphore()

    def greet(index, carry):
        pl.semaphore_signal(barrier, inc=1, device_id=target(index), device_id_type=MESH)
        return carry

    lax.fori_loop(1, 128, greet, 0)

    def group_step(group, carry):
        @pl.when(group == 0)
        def _():
            load(0).wait()

        @pl.when(group > 0)
        def _():
            load(group).wait()

        def filter_column(index, carry):
            weights = [jnp.broadcast_to(taps[pl.ds(t, 1), pl.ds(pl.multiple_of(index * LANES, LANES), LANES)], (16, LANES)) for t in range(TAPS)]
            for part in range(2):
                frames = []
                for frame in range(GROUP + TAPS - 1):
                    start = pl.multiple_of((group * GROUP + frame) * CH + index * LANES, LANES)
                    frames.append(volt[part, :, pl.ds(start, LANES)].astype(jnp.float32))
                for spec in range(GROUP):
                    total = weights[0] * frames[spec]
                    for tap in range(1, TAPS):
                        total = total + weights[tap] * frames[spec + tap]
                    filt[part, spec, index] = total.astype(jnp.bfloat16)
            return carry

        lax.fori_loop(0, COLS, filter_column, 0)

        for spec in range(GROUP):
            for half in range(2):
                rows = slice(half * 8, half * 8 + 8)
                values = []
                for index in range(COLS):
                    values.append(tuple(filt[part, spec, index].astype(jnp.float32)[rows] for part in range(2)))
                for index, (real, imag) in enumerate(fft_columns(values)):
                    cos, sin = turn_cos[index], turn_sin[index]
                    place = pl.ds(half * LANES + spec * COLS + index, 8, stride=2 * LANES)
                    z_real[place, :] = real * cos - imag * sin
                    z_imag[place, :] = real * sin + imag * cos

        def last_step(block, carry):
            rows = pl.ds(pl.multiple_of(block * 256, 256), 256)
            both = jnp.concatenate([z_real[rows, :], z_imag[rows, :]], axis=1)
            high = both.astype(jnp.bfloat16)
            low = (both - high.astype(jnp.float32)).astype(jnp.bfloat16)
            dims = (((1,), (1,)), ((), ()))
            total = lax.dot_general(dft_high[...], high, dims, preferred_element_type=jnp.float32)
            total = total + lax.dot_general(dft_low[...], high, dims, preferred_element_type=jnp.float32)
            total = total + lax.dot_general(dft_high[...], low, dims, preferred_element_type=jnp.float32)
            for part in range(2):
                for half in range(2):
                    piece = total[part * 128:part * 128 + 128, half * 128:half * 128 + 128]
                    wide[pl.ds(block * 4 + part * 2 + half, 128, stride=32), :] = piece
            return carry

        lax.fori_loop(0, 8, last_step, 0)

        def narrow(index, carry):
            rows = pl.ds(pl.multiple_of(index * 256, 256), 256)
            pieces[group, pl.ds(index * 8, 8)] = wide[rows, :].astype(jnp.bfloat16).reshape(8, 32, LANES)
            return carry

        lax.fori_loop(0, 16, narrow, 0)

        @pl.when(group == 0)
        def _():
            pl.semaphore_wait(barrier, 127)

        def send(index, carry):
            freq, blk = target(index)
            pltpu.make_async_remote_copy(
                src_ref=pieces.at[group, freq * 8 + blk],
                dst_ref=out.at[group, me],
                send_sem=send_sem.at[group],
                recv_sem=recv_sem.at[group],
                device_id=(freq, blk),
                device_id_type=MESH,
            ).start()
            return carry

        lax.fori_loop(1, 128, send, 0)
        pltpu.make_async_copy(pieces.at[group, me], out.at[group, me], own_sem.at[group]).start()
        return carry

    lax.fori_loop(0, GROUPS, group_step, 0)

    def finish(group, carry):
        pltpu.make_async_copy(pieces.at[group, me], out.at[group, me], own_sem.at[group]).wait()
        others = pl.ds(0, 127)
        pltpu.make_async_copy(pieces.at[group, others], out.at[group, others], send_sem.at[group]).wait()
        pltpu.make_async_copy(pieces.at[group, others], out.at[group, others], recv_sem.at[group]).wait()
        return carry

    lax.fori_loop(0, GROUPS, finish, 0)


def tables():
    rows = np.arange(COLS)[:, None] * np.arange(LANES)[None, :]
    angles = -2.0 * np.pi * rows / CH
    cos = np.repeat(np.cos(angles)[:, None, :], 8, 1) / 64
    sin = np.repeat(np.sin(angles)[:, None, :], 8, 1) / 64
    steps = np.arange(LANES)
    turn = -2.0 * np.pi * (steps[:, None] * steps[None, :] % LANES) / LANES
    dft = np.block([[np.cos(turn), -np.sin(turn)], [np.sin(turn), np.cos(turn)]]).astype(np.float32)
    high = jnp.asarray(dft).astype(jnp.bfloat16)
    low = (jnp.asarray(dft) - high.astype(jnp.float32)).astype(jnp.bfloat16)
    return jnp.asarray(cos, jnp.float32), jnp.asarray(sin, jnp.float32), high, low


def whole(shape):
    return pl.BlockSpec(shape, lambda *_: (0,) * len(shape))


def channelize(voltages, pfb_taps):
    cos, sin, high, low = tables()
    inputs = [pfb_taps, cos, sin, high, low]
    return pl.pallas_call(
        channelize_kernel,
        out_shape=jax.ShapeDtypeStruct((GROUPS, 128, 32, LANES), jnp.bfloat16),
        in_specs=[pl.BlockSpec(memory_space=pl.ANY)] + [pl.BlockSpec(memory_space=pltpu.VMEM)] * 5,
        out_specs=pl.BlockSpec(memory_space=pl.ANY),
        scratch_shapes=[
            pltpu.VMEM(voltages.shape, jnp.bfloat16),
            pltpu.VMEM((2, GROUP, COLS, 16, LANES), jnp.bfloat16),
            pltpu.VMEM((2048, LANES), jnp.float32),
            pltpu.VMEM((2048, LANES), jnp.float32),
            pltpu.VMEM((4096, LANES), jnp.float32),
            pltpu.VMEM((GROUPS, 128, 32, LANES), jnp.bfloat16),
        ] + [pltpu.SemaphoreType.DMA((GROUPS,))] * 4,
        compiler_params=pltpu.CompilerParams(vmem_limit_bytes=48 * 2**20, collective_id=0, has_side_effects=True),
        cost_estimate=pl.CostEstimate(flops=10**10, bytes_accessed=16 * 2**20, transcendentals=0),
    )(voltages, *inputs)


def correlate_kernel(lag_table, arrived, order, spread, near, far, natural, rows_x, rows_y, tiles, far_tiles, sems):
    blk = lax.axis_index("blk")
    freq = lax.axis_index("freq")
    dims = (((1,), (1,)), ((), ()))
    barrier = pltpu.get_barrier_semaphore()
    col, side = lax.rem(blk, 4), blk // 4

    def target(index):
        step = lax.rem(index * 3 + 1, 8)
        return step, lax.rem(side + step // 4, 2) * 4 + lax.rem(col + lax.rem(step, 4), 4)

    for step in range(1, 8):
        pl.semaphore_signal(barrier, inc=1, device_id=(freq, lax.rem(blk + step, 8)), device_id_type=MESH)

    def unshuffle(index, carry):
        source = pl.ds(pl.multiple_of(index * 8, 8), 8)
        for pair in range(2):
            lanes = jnp.concatenate([arrived[2 * pair + step, source].reshape(256, LANES) for step in range(2)], axis=1)
            sorted_rows = jnp.dot(spread[...], lanes, preferred_element_type=jnp.float32).astype(jnp.bfloat16)
            for member in range(8):
                for part in range(2):
                    start = member * 32 + part * 16
                    natural[member, pl.ds(pl.multiple_of(index * 16, 16), 16), part * 512 + pair * 256:part * 512 + pair * 256 + 256] = sorted_rows[start:start + 16]
        return carry

    lax.fori_loop(0, 16, unshuffle, 0)
    members = lax.broadcasted_iota(jnp.int32, (256, 256), 1)
    for member in range(8):
        chosen = (order[:, member:member + 1] == members).astype(jnp.bfloat16)
        picked = jnp.dot(chosen, natural[member], preferred_element_type=jnp.float32)
        rows_x[member] = picked.astype(jnp.bfloat16)
        rows_y[member, :, :512] = picked[:, 512:].astype(jnp.bfloat16)
        rows_y[member, :, 512:] = (-picked[:, :512]).astype(jnp.bfloat16)
    pl.semaphore_wait(barrier, 7)

    def tile(left, other, part):
        value = lax.dot_general((rows_x, rows_y)[part][left], rows_x[other], dims, preferred_element_type=jnp.float32)
        return (value * (1.0 / 512)).astype(jnp.bfloat16)

    def post(is_own, dest, source, place, send, receive, own):
        @pl.when(is_own)
        def _():
            pltpu.make_async_copy(source, place, own).start()

        @pl.when(jnp.logical_not(is_own))
        def _():
            pltpu.make_async_remote_copy(src_ref=source, dst_ref=place, send_sem=send, recv_sem=receive, device_id=(freq, dest), device_id_type=MESH).start()

    parity = lax.rem(blk, 2)

    def near_step(index, carry):
        slot, turn = index // 8, lax.rem(index, 8)
        step, dest = target(turn)
        other = lax.rem(dest + lag_table[slot], 8)
        for part in range(2):
            tiles[index, part] = tile(dest, other, part)
            post(step == 0, dest, tiles.at[index, part], near.at[blk, slot, part], sems.at[0], sems.at[1], sems.at[2])
        return carry

    lax.fori_loop(0, 32, near_step, 0)

    def far_step(index, carry):
        dest = parity * 4 + lax.rem(col + index, 4)
        for part in range(2):
            far_tiles[index, part] = tile(dest, lax.rem(dest + 4, 8), part)
            post(dest == blk, dest, far_tiles.at[index, part], far.at[blk // 2, part], sems.at[3], sems.at[4], sems.at[5])
        return carry

    lax.fori_loop(0, 4, far_step, 0)

    own_near = pltpu.make_async_copy(tiles.at[pl.ds(0, 4)], near.at[0], sems.at[2])
    own_near.wait()
    for sem in (0, 1):
        pltpu.make_async_copy(near.at[pl.ds(0, 7)], near.at[pl.ds(0, 7)], sems.at[sem]).wait()
    has_own = parity == side

    @pl.when(has_own)
    def _():
        pltpu.make_async_copy(far_tiles.at[0], far.at[0], sems.at[5]).wait()
        for sem in (3, 4):
            pltpu.make_async_copy(far_tiles.at[pl.ds(0, 3)], far.at[pl.ds(0, 3)], sems.at[sem]).wait()

    @pl.when(jnp.logical_not(has_own))
    def _():
        for sem in (3, 4):
            pltpu.make_async_copy(far_tiles, far, sems.at[sem]).wait()


def correlate(arrived, order, lag_table):
    inputs = [arrived, order, spread_table()]
    return pl.pallas_call(
        correlate_kernel,
        out_shape=(
            jax.ShapeDtypeStruct((8, 4, 2, 256, 256), jnp.bfloat16),
            jax.ShapeDtypeStruct((4, 2, 256, 256), jnp.bfloat16),
        ),
        in_specs=[pl.BlockSpec(memory_space=pltpu.SMEM)] + [pl.BlockSpec(memory_space=pltpu.VMEM)] * 3,
        out_specs=(pl.BlockSpec(memory_space=pl.ANY), pl.BlockSpec(memory_space=pl.ANY)),
        scratch_shapes=[pltpu.VMEM((8, 256, 1024), jnp.bfloat16)] * 3
        + [pltpu.VMEM((32, 2, 256, 256), jnp.bfloat16), pltpu.VMEM((4, 2, 256, 256), jnp.bfloat16), pltpu.SemaphoreType.DMA((6,))],
        compiler_params=pltpu.CompilerParams(vmem_limit_bytes=48 * 2**20, collective_id=1, has_side_effects=True),
        cost_estimate=pl.CostEstimate(flops=10**10, bytes_accessed=16 * 2**20, transcendentals=0),
    )(lag_table, *inputs)


def per_device(voltages, pfb_taps, order_table, lag_table):
    orders = lax.all_gather(order_table, "blk", axis=0, tiled=True)
    arrived = channelize(voltages, pfb_taps)
    near, far = correlate(arrived, orders.T, lag_table)
    return near[:, None], far[:, None]


def spread_table():
    table = np.zeros((256, 256), np.float32)
    for source in range(8):
        for row in range(16):
            for half in range(2):
                table[row * 16 + source * 2 + half, source * 32 + row * 2 + half] = 1
    return jnp.asarray(table).astype(jnp.bfloat16)


def solution(mesh):
    placed = (P(None, ("freq", "blk"), None), P(), P("blk", None), P())
    return jax.shard_map(
        per_device,
        mesh=mesh,
        in_specs=placed,
        out_specs=(P("freq", "blk", None, None, None, None), P("freq", "blk", None, None, None)),
        check_vma=False,
    )
```

```python
import functools
import math

import jax
import jax.numpy as jnp
import numpy as np
from jax import lax
from jax.experimental import pallas as pl
from jax.experimental.pallas import tpu as pltpu
from jax.sharding import PartitionSpec as P

CH = 4096
TAPS = 16
SPECTRA = 16
COLS = 32
LANES = 128
GROUP = 4
GROUPS = 4


def complex_mul(value, turn):
    real, imag = value
    cos, sin = float(turn.real), float(turn.imag)
    if abs(sin) < 1e-12 and abs(cos - 1) < 1e-12:
        return value
    if abs(cos) < 1e-12 and abs(sin + 1) < 1e-12:
        return (imag, -real)
    if abs(cos + sin) < 1e-12:
        return ((real + imag) * cos, (imag - real) * cos)
    if abs(cos - sin) < 1e-12:
        return ((real - imag) * cos, (real + imag) * cos)
    return (real * cos - imag * sin, real * sin + imag * cos)


def fft_list(values):
    count = len(values)
    if count == 1:
        return values
    if count == 2:
        (ar, ai), (br, bi) = values
        return [(ar + br, ai + bi), (ar - br, ai - bi)]
    if count == 4:
        even = fft_list([values[0], values[2]])
        odd = fft_list([values[1], values[3]])
    else:
        even = fft_list(values[0::2])
        odd = fft_list(values[1::2])
    half = count // 2
    low, high = [], []
    for index in range(half):
        turned = complex_mul(odd[index], np.exp(-2j * np.pi * index / count))
        base = even[index]
        low.append((base[0] + turned[0], base[1] + turned[1]))
        high.append((base[0] - turned[0], base[1] - turned[1]))
    return low + high


def fft_columns(values):
    sections = []
    for low in range(8):
        parts = fft_list([values[8 * high + low] for high in range(4)])
        sections.append([complex_mul(part, np.exp(-2j * np.pi * low * index / 32)) for index, part in enumerate(parts)])
    result = [None] * 32
    for index in range(4):
        parts = fft_list([sections[low][index] for low in range(8)])
        for high in range(8):
            result[index + 4 * high] = parts[high]
    return result


MESH = pl.DeviceIdType.MESH
CONTRACT_LAST = (((1,), (1,)), ((), ()))


def position():
    freq = lax.axis_index("freq")
    blk = lax.axis_index("blk")
    return (lax.rem(blk, 4), lax.rem(freq // 2, 2) * 2 + blk // 4, freq // 4, lax.rem(freq, 2))


def mesh_ids(col, row, layer, core):
    return (layer * 4 + (row // 2) * 2 + core, lax.rem(row, 2) * 4 + col)


def correlator_kernel(
    volt_far, order_row, taps_far, cos_far, sin_far, high_far, low_far, spread_far,
    near, far,
    volt, taps, turn_cos, turn_sin, dft_high, dft_low, spread,
    filt, z_real, z_imag, wide, pieces, arrived, own_order, orders, chosen, natural, rows, tiles, far_tiles,
    load_sem, const_sem, send_sem, recv_sem, own_sem, order_sem, tile_sem,
):
    def load(group):
        first = 0 if isinstance(group, int) else pl.multiple_of((group * GROUP + TAPS - 1) * CH, LANES)
        size = (GROUP + TAPS - 1) * CH if isinstance(group, int) else GROUP * CH
        place = (slice(None), slice(None), pl.ds(first, size))
        return pltpu.make_async_copy(volt_far.at[place], volt.at[place], load_sem.at[group])

    constants = [
        pltpu.make_async_copy(source, place, const_sem.at[index])
        for index, (source, place) in enumerate(
            ((taps_far, taps), (cos_far, turn_cos), (sin_far, turn_sin), (high_far, dft_high), (low_far, dft_low), (spread_far, spread))
        )
    ]
    constants[0].start()
    load(0).start()
    for constant in constants[1:]:
        constant.start()
    for later in range(1, GROUPS):
        load(jnp.int32(later)).start()

    col, row, layer, core = position()
    freq, blk = mesh_ids(col, row, layer, core)
    me = freq * 8 + blk
    side = blk // 4
    parity = lax.rem(blk, 2)

    def target(index):
        step = lax.rem(index * 75, 128)
        return mesh_ids(
            lax.rem(col + lax.rem(step, 4), 4),
            lax.rem(row + lax.rem(step // 4, 4), 4),
            lax.rem(layer + lax.rem(step // 16, 4), 4),
            lax.rem(core + step // 64, 2),
        )

    barrier = pltpu.get_barrier_semaphore()

    def greet(index, carry):
        pl.semaphore_signal(barrier, inc=1, device_id=target(index), device_id_type=MESH)
        return carry

    lax.fori_loop(1, 128, greet, 0)
    own_order[...] = jnp.broadcast_to(order_row[...], (8, 256))
    for constant in constants:
        constant.wait()

    def order_copy(step):
        return pltpu.make_async_remote_copy(
            src_ref=own_order,
            dst_ref=orders.at[blk],
            send_sem=order_sem.at[0],
            recv_sem=order_sem.at[1],
            device_id=(freq, lax.rem(blk + step, 8)),
            device_id_type=MESH,
        )

    def group_step(group, carry):
        @pl.when(group == 0)
        def _():
            load(0).wait()

        @pl.when(group > 0)
        def _():
            load(group).wait()

        def filter_column(index, carry):
            weights = [jnp.broadcast_to(taps[pl.ds(t, 1), pl.ds(pl.multiple_of(index * LANES, LANES), LANES)], (16, LANES)) for t in range(TAPS)]
            for part in range(2):
                frames = []
                for frame in range(GROUP + TAPS - 1):
                    start = pl.multiple_of((group * GROUP + frame) * CH + index * LANES, LANES)
                    frames.append(volt[part, :, pl.ds(start, LANES)].astype(jnp.float32))
                for spec in range(GROUP):
                    total = weights[0] * frames[spec]
                    for tap in range(1, TAPS):
                        total = total + weights[tap] * frames[spec + tap]
                    filt[part, spec, index] = total.astype(jnp.bfloat16)
            return carry

        lax.fori_loop(0, COLS, filter_column, 0)

        for spec in range(GROUP):
            for half in range(2):
                rows_half = slice(half * 8, half * 8 + 8)
                values = []
                for index in range(COLS):
                    values.append(tuple(filt[part, spec, index].astype(jnp.float32)[rows_half] for part in range(2)))
                for index, (real, imag) in enumerate(fft_columns(values)):
                    cos, sin = turn_cos[index], turn_sin[index]
                    place = pl.ds(half * LANES + spec * COLS + index, 8, stride=2 * LANES)
                    z_real[place, :] = real * cos - imag * sin
                    z_imag[place, :] = real * sin + imag * cos

        def last_step(block, carry):
            block_rows = pl.ds(pl.multiple_of(block * 256, 256), 256)
            both = jnp.concatenate([z_real[block_rows, :], z_imag[block_rows, :]], axis=1)
            high = both.astype(jnp.bfloat16)
            low = (both - high.astype(jnp.float32)).astype(jnp.bfloat16)
            total = lax.dot_general(dft_high[...], high, CONTRACT_LAST, preferred_element_type=jnp.float32)
            total = total + lax.dot_general(dft_low[...], high, CONTRACT_LAST, preferred_element_type=jnp.float32)
            total = total + lax.dot_general(dft_high[...], low, CONTRACT_LAST, preferred_element_type=jnp.float32)
            for part in range(2):
                for half in range(2):
                    piece = total[part * 128:part * 128 + 128, half * 128:half * 128 + 128]
                    wide[pl.ds(block * 4 + part * 2 + half, 128, stride=32), :] = piece
            return carry

        lax.fori_loop(0, 8, last_step, 0)

        def narrow(index, carry):
            wide_rows = pl.ds(pl.multiple_of(index * 256, 256), 256)
            pieces[group, pl.ds(index * 8, 8)] = wide[wide_rows, :].astype(jnp.bfloat16).reshape(8, 32, LANES)
            return carry

        lax.fori_loop(0, 16, narrow, 0)

        @pl.when(group == 0)
        def _():
            pl.semaphore_wait(barrier, 127)
            for step in range(1, 8):
                order_copy(step).start()

        def send(index, carry):
            other_freq, other_blk = target(index)
            pltpu.make_async_remote_copy(
                src_ref=pieces.at[group, other_freq * 8 + other_blk],
                dst_ref=arrived.at[group, me],
                send_sem=send_sem.at[group],
                recv_sem=recv_sem.at[group],
                device_id=(other_freq, other_blk),
                device_id_type=MESH,
            ).start()
            return carry

        lax.fori_loop(1, 128, send, 0)
        pltpu.make_async_copy(pieces.at[group, me], arrived.at[group, me], own_sem.at[group]).start()
        return carry

    lax.fori_loop(0, GROUPS, group_step, 0)

    orders[blk] = own_order[...]
    for sem in range(2):
        pltpu.make_async_copy(orders.at[pl.ds(0, 7)], orders.at[pl.ds(0, 7)], order_sem.at[sem]).wait()
    members = lax.broadcasted_iota(jnp.int32, (256, 256), 0)
    for member in range(8):
        flags = (orders[member, 0:1, :] == members).astype(jnp.float32)
        chosen[member] = flags.T.astype(jnp.bfloat16)

    def take_group(group, carry):
        others = pl.ds(0, 127)
        pltpu.make_async_copy(pieces.at[group, me], arrived.at[group, me], own_sem.at[group]).wait()
        pltpu.make_async_copy(pieces.at[group, others], arrived.at[group, others], recv_sem.at[group]).wait()

        def unshuffle(index, carry):
            lanes = jnp.concatenate(
                [arrived[group, pl.ds(pl.multiple_of(index * 16 + step * 8, 8), 8)].reshape(256, LANES) for step in range(2)], axis=1
            )
            sorted_rows = jnp.dot(spread[...], lanes, preferred_element_type=jnp.float32).astype(jnp.bfloat16)
            for member in range(8):
                for part in range(2):
                    start = member * 32 + part * 16
                    for step in range(2):
                        place = pl.ds(pl.multiple_of(index * 32 + step * 16, 16), 16)
                        natural[member, place, part * LANES:part * LANES + LANES] = sorted_rows[start:start + 16, step * LANES:step * LANES + LANES]
            return carry

        lax.fori_loop(0, 8, unshuffle, 0)

        def arrange(member, carry):
            picked = jnp.dot(chosen[member], natural[member], preferred_element_type=jnp.float32).astype(jnp.bfloat16)
            for part in range(2):
                rows[member, part * GROUPS + group] = picked[:, part * LANES:part * LANES + LANES]
            return carry

        lax.fori_loop(0, 8, arrange, 0)
        return carry

    lax.fori_loop(0, GROUPS, take_group, 0)

    def side_of(member, part):
        return jnp.concatenate([rows[member, part * GROUPS + group] for group in range(GROUPS)], axis=1)

    def product(left, right):
        return lax.dot_general(left, right, CONTRACT_LAST, preferred_element_type=jnp.float32)

    def correlate(member, other):
        left_real, left_imag = side_of(member, 0), side_of(member, 1)
        right_real, right_imag = side_of(other, 0), side_of(other, 1)
        real = product(left_real, right_real) + product(left_imag, right_imag)
        imag = product(left_imag, right_real) - product(left_real, right_imag)
        return real * (1.0 / 512), imag * (1.0 / 512)

    def post(is_own, dest, source, place, send, receive, own):
        @pl.when(is_own)
        def _():
            pltpu.make_async_copy(source, place, own).start()

        @pl.when(jnp.logical_not(is_own))
        def _():
            pltpu.make_async_remote_copy(
                src_ref=source, dst_ref=place, send_sem=send, recv_sem=receive, device_id=(freq, dest), device_id_type=MESH
            ).start()

    def turn_target(turn):
        step = lax.rem(turn * 3 + 1, 8)
        return step, lax.rem(side + step // 4, 2) * 4 + lax.rem(col + lax.rem(step, 4), 4)

    def near_step(index, carry):
        lag = index // 8 + 1
        step, dest = turn_target(lax.rem(index, 8))
        values = correlate(dest, lax.rem(dest + lag, 8))
        for part in range(2):
            place = (lag - 1) * 2 + part
            tiles[dest, place] = values[part].astype(jnp.bfloat16)
            post(step == 0, dest, tiles.at[dest, place], near.at[blk, place], tile_sem.at[0], tile_sem.at[1], tile_sem.at[2])
        return carry

    lax.fori_loop(0, 24, near_step, 0)

    def packed_step(index, carry):
        step, dest = turn_target(index)
        real, imag = correlate(dest, dest)
        down = lax.broadcasted_iota(jnp.int32, (256, 256), 0)
        across = lax.broadcasted_iota(jnp.int32, (256, 256), 1)
        tiles[dest, 6] = jnp.where(down >= across, real, imag).astype(jnp.bfloat16)
        post(step == 0, dest, tiles.at[dest, 6], near.at[blk, 6], tile_sem.at[0], tile_sem.at[1], tile_sem.at[2])
        return carry

    lax.fori_loop(0, 8, packed_step, 0)

    def far_step(index, carry):
        dest = parity * 4 + lax.rem(col + index, 4)
        values = correlate(dest, lax.rem(dest + 4, 8))
        for part in range(2):
            far_tiles[index, part] = values[part].astype(jnp.bfloat16)
            post(dest == blk, dest, far_tiles.at[index, part], far.at[blk // 2, part], tile_sem.at[3], tile_sem.at[4], tile_sem.at[5])
        return carry

    lax.fori_loop(0, 4, far_step, 0)

    def finish(group, carry):
        others = pl.ds(0, 127)
        pltpu.make_async_copy(pieces.at[group, others], arrived.at[group, others], send_sem.at[group]).wait()
        return carry

    lax.fori_loop(0, GROUPS, finish, 0)
    pltpu.make_async_copy(tiles.at[0], near.at[0], tile_sem.at[2]).wait()
    for sem in (0, 1):
        pltpu.make_async_copy(tiles.at[pl.ds(0, 7)], near.at[pl.ds(0, 7)], tile_sem.at[sem]).wait()
    has_own = parity == side

    @pl.when(has_own)
    def _():
        pltpu.make_async_copy(far_tiles.at[0], far.at[0], tile_sem.at[5]).wait()
        for sem in (3, 4):
            pltpu.make_async_copy(far_tiles.at[pl.ds(0, 3)], far.at[pl.ds(0, 3)], tile_sem.at[sem]).wait()

    @pl.when(jnp.logical_not(has_own))
    def _():
        for sem in (3, 4):
            pltpu.make_async_copy(far_tiles, far, tile_sem.at[sem]).wait()


def tables():
    rows = np.arange(COLS)[:, None] * np.arange(LANES)[None, :]
    angles = -2.0 * np.pi * rows / CH
    cos = np.repeat(np.cos(angles)[:, None, :], 8, 1) / 64
    sin = np.repeat(np.sin(angles)[:, None, :], 8, 1) / 64
    steps = np.arange(LANES)
    turn = -2.0 * np.pi * (steps[:, None] * steps[None, :] % LANES) / LANES
    dft = np.block([[np.cos(turn), -np.sin(turn)], [np.sin(turn), np.cos(turn)]]).astype(np.float32)
    high = jnp.asarray(dft).astype(jnp.bfloat16)
    low = (jnp.asarray(dft) - high.astype(jnp.float32)).astype(jnp.bfloat16)
    return jnp.asarray(cos, jnp.float32), jnp.asarray(sin, jnp.float32), high, low


def make_tiles(voltages, pfb_taps, order_table):
    cos, sin, high, low = tables()
    constants = [pfb_taps, cos, sin, high, low, spread_table()]
    anywhere = pl.BlockSpec(memory_space=pl.ANY)
    return pl.pallas_call(
        correlator_kernel,
        out_shape=(
            jax.ShapeDtypeStruct((8, 7, 256, 256), jnp.bfloat16),
            jax.ShapeDtypeStruct((4, 2, 256, 256), jnp.bfloat16),
        ),
        in_specs=[anywhere, pl.BlockSpec(memory_space=pltpu.VMEM)] + [pl.BlockSpec(memory_space=pltpu.HBM)] * 6,
        out_specs=(anywhere, anywhere),
        scratch_shapes=[pltpu.VMEM(voltages.shape, jnp.bfloat16)]
        + [pltpu.VMEM(value.shape, value.dtype) for value in constants]
        + [
            pltpu.VMEM((2, GROUP, COLS, 16, LANES), jnp.bfloat16),
            pltpu.VMEM((2048, LANES), jnp.float32),
            pltpu.VMEM((2048, LANES), jnp.float32),
            pltpu.VMEM((4096, LANES), jnp.float32),
            pltpu.VMEM((GROUPS, 128, 32, LANES), jnp.bfloat16),
            pltpu.VMEM((GROUPS, 128, 32, LANES), jnp.bfloat16),
            pltpu.VMEM((8, 256), jnp.int32),
            pltpu.VMEM((8, 8, 256), jnp.int32),
            pltpu.VMEM((8, 256, 256), jnp.bfloat16),
            pltpu.VMEM((8, 256, 256), jnp.bfloat16),
            pltpu.VMEM((8, 8, 256, LANES), jnp.bfloat16),
            pltpu.VMEM((8, 7, 256, 256), jnp.bfloat16),
            pltpu.VMEM((4, 2, 256, 256), jnp.bfloat16),
            pltpu.SemaphoreType.DMA((GROUPS,)),
            pltpu.SemaphoreType.DMA((6,)),
            pltpu.SemaphoreType.DMA((GROUPS,)),
            pltpu.SemaphoreType.DMA((GROUPS,)),
            pltpu.SemaphoreType.DMA((GROUPS,)),
            pltpu.SemaphoreType.DMA((2,)),
            pltpu.SemaphoreType.DMA((6,)),
        ],
        compiler_params=pltpu.CompilerParams(vmem_limit_bytes=42 * 2**20, collective_id=0, has_side_effects=True),
        cost_estimate=pl.CostEstimate(flops=10**10, bytes_accessed=16 * 2**20, transcendentals=0),
    )(voltages, order_table, *constants)


def arrange_kernel(lag_table, near, far, visibility, far_visibility):
    for slot in range(4):
        lag = lag_table[slot]

        @pl.when(lag > 0)
        def _(slot=slot, lag=lag):
            for part in range(2):
                visibility[0, 0, slot, part] = near[0, (lag - 1) * 2 + part]

        @pl.when(lag == 0)
        def _(slot=slot):
            packed = near[0, 6].astype(jnp.float32)
            turned = packed.T
            down = lax.broadcasted_iota(jnp.int32, (256, 256), 0)
            across = lax.broadcasted_iota(jnp.int32, (256, 256), 1)
            visibility[0, 0, slot, 0] = jnp.where(down >= across, packed, turned).astype(jnp.bfloat16)
            mirrored = jnp.where(down > across, -turned, 0.0)
            visibility[0, 0, slot, 1] = jnp.where(down < across, packed, mirrored).astype(jnp.bfloat16)

    far_visibility[0, 0, 0] = far[0, 0]


def arrange(near, far, lag_table):
    return pl.pallas_call(
        arrange_kernel,
        grid=(8,),
        out_shape=(
            jax.ShapeDtypeStruct((8, 1, 4, 2, 256, 256), jnp.bfloat16),
            jax.ShapeDtypeStruct((4, 1, 2, 256, 256), jnp.bfloat16),
        ),
        in_specs=[
            pl.BlockSpec(memory_space=pltpu.SMEM),
            pl.BlockSpec((1, 7, 256, 256), lambda out: (out, 0, 0, 0)),
            pl.BlockSpec((1, 1, 256, 256), lambda out: (out // 2, out % 2, 0, 0)),
        ],
        out_specs=(
            pl.BlockSpec((1, 1, 4, 2, 256, 256), lambda out: (out, 0, 0, 0, 0, 0)),
            pl.BlockSpec((1, 1, 1, 256, 256), lambda out: (out // 2, 0, out % 2, 0, 0)),
        ),
        compiler_params=pltpu.CompilerParams(vmem_limit_bytes=16 * 2**20),
    )(lag_table, near, far)


def per_device(voltages, pfb_taps, order_table, lag_table):
    near, far = make_tiles(voltages, pfb_taps, order_table)
    return arrange(near, far, lag_table)


def spread_table():
    table = np.zeros((256, 256), np.float32)
    for source in range(8):
        for row in range(16):
            for half in range(2):
                table[row * 16 + source * 2 + half, source * 32 + row * 2 + half] = 1
    return jnp.asarray(table).astype(jnp.bfloat16)


def solution(mesh):
    placed = (P(None, ("freq", "blk"), None), P(), P("blk", None), P())
    return jax.shard_map(
        per_device,
        mesh=mesh,
        in_specs=placed,
        out_specs=(P("freq", "blk", None, None, None, None), P("freq", "blk", None, None, None)),
        check_vma=False,
    )
```

```python
import functools
import math

import jax
import jax.numpy as jnp
import numpy as np
from jax import lax
from jax.experimental import pallas as pl
from jax.experimental.pallas import tpu as pltpu
from jax.sharding import PartitionSpec as P

CH = 4096
TAPS = 16
SPECTRA = 16
COLS = 32
LANES = 128
GROUP = 4
GROUPS = 4
Z_STRIDE = 264
WIDE_STRIDE = 40


def complex_mul(value, turn):
    real, imag = value
    cos, sin = float(turn.real), float(turn.imag)
    if abs(sin) < 1e-12 and abs(cos - 1) < 1e-12:
        return value
    if abs(cos) < 1e-12 and abs(sin + 1) < 1e-12:
        return (imag, -real)
    if abs(cos + sin) < 1e-12:
        return ((real + imag) * cos, (imag - real) * cos)
    if abs(cos - sin) < 1e-12:
        return ((real - imag) * cos, (real + imag) * cos)
    return (real * cos - imag * sin, real * sin + imag * cos)


def fft_list(values):
    count = len(values)
    if count == 1:
        return values
    if count == 2:
        (ar, ai), (br, bi) = values
        return [(ar + br, ai + bi), (ar - br, ai - bi)]
    if count == 4:
        even = fft_list([values[0], values[2]])
        odd = fft_list([values[1], values[3]])
    else:
        even = fft_list(values[0::2])
        odd = fft_list(values[1::2])
    half = count // 2
    low, high = [], []
    for index in range(half):
        turned = complex_mul(odd[index], np.exp(-2j * np.pi * index / count))
        base = even[index]
        low.append((base[0] + turned[0], base[1] + turned[1]))
        high.append((base[0] - turned[0], base[1] - turned[1]))
    return low + high


def fft_columns(values):
    sections = []
    for low in range(8):
        parts = fft_list([values[8 * high + low] for high in range(4)])
        sections.append([complex_mul(part, np.exp(-2j * np.pi * low * index / 32)) for index, part in enumerate(parts)])
    result = [None] * 32
    for index in range(4):
        parts = fft_list([sections[low][index] for low in range(8)])
        for high in range(8):
            result[index + 4 * high] = parts[high]
    return result


MESH = pl.DeviceIdType.MESH
CONTRACT_LAST = (((1,), (1,)), ((), ()))


def position():
    freq = lax.axis_index("freq")
    blk = lax.axis_index("blk")
    return (lax.rem(blk, 4), lax.rem(freq // 2, 2) * 2 + blk // 4, freq // 4, lax.rem(freq, 2))


def mesh_ids(col, row, layer, core):
    return (layer * 4 + (row // 2) * 2 + core, lax.rem(row, 2) * 4 + col)


def correlator_kernel(
    volt_far, order_row, taps, numbers,
    near, far,
    volt, turn_cos, turn_sin, dft_high, dft_low, spread,
    filt, z_real, z_imag, wide, pieces, arrived, own_order, orders, chosen, natural, rows, tiles, far_tiles,
    load_sem, send_sem, recv_sem, own_sem, order_sem, tile_sem,
):
    def load(group):
        first = 0 if isinstance(group, int) else pl.multiple_of((group * GROUP + TAPS - 1) * CH, LANES)
        size = (GROUP + TAPS - 1) * CH if isinstance(group, int) else GROUP * CH
        place = (slice(None), slice(None), pl.ds(first, size))
        return pltpu.make_async_copy(volt_far.at[place], volt.at[place], load_sem.at[group])

    load(0).start()
    for later in range(1, GROUPS):
        load(jnp.int32(later)).start()

    col, row, layer, core = position()
    freq, blk = mesh_ids(col, row, layer, core)
    me = freq * 8 + blk
    side = blk // 4
    channel = col * 2 + side

    def visit_others(visit):
        cols = [lax.rem(col + step, 4) for step in range(4)]

        def visit_plane(index, carry):
            new_row = lax.rem(row + lax.rem(index, 4), 4)
            new_layer = lax.rem(layer + lax.rem(lax.div(index, 4), 4), 4)
            new_core = lax.rem(core + lax.div(index, 16), 2)
            other_freq = new_layer * 4 + lax.div(new_row, 2) * 2 + new_core
            other_side = lax.rem(new_row, 2)

            @pl.when(index > 0)
            def _():
                visit(other_freq, other_side, cols[0])

            for step in range(1, 4):
                visit(other_freq, other_side, cols[step])
            return carry

        lax.fori_loop(0, 32, visit_plane, 0)

    barrier = pltpu.get_barrier_semaphore()

    def greet(other_freq, other_side, other_col):
        pl.semaphore_signal(barrier, inc=1, device_id=(other_freq, other_side * 4 + other_col), device_id_type=MESH)

    visit_others(greet)
    own_order[...] = jnp.broadcast_to(order_row[...], (8, 256))
    for index in range(COLS):
        turn_cos[index] = jnp.broadcast_to(numbers[index:index + 1, :], (8, LANES))
        turn_sin[index] = jnp.broadcast_to(numbers[COLS + index:COLS + index + 1, :], (8, LANES))
    dft = jnp.concatenate([numbers[2 * COLS:2 * COLS + 256, :], numbers[2 * COLS + 256:2 * COLS + 512, :]], axis=1)
    dft_high[...] = dft.astype(jnp.bfloat16)
    dft_low[...] = (dft - dft.astype(jnp.bfloat16).astype(jnp.float32)).astype(jnp.bfloat16)
    sorted_row = lax.broadcasted_iota(jnp.int32, (256, 256), 0)
    came_row = lax.broadcasted_iota(jnp.int32, (256, 256), 1)
    wanted = jnp.bitwise_and(sorted_row, 14) * 16 + lax.shift_right_logical(sorted_row, 4) * 2 + jnp.bitwise_and(sorted_row, 1)
    spread[...] = (wanted == came_row).astype(jnp.float32).astype(jnp.bfloat16)

    def order_copy(step):
        return pltpu.make_async_remote_copy(
            src_ref=own_order,
            dst_ref=orders.at[blk],
            send_sem=order_sem.at[0],
            recv_sem=order_sem.at[1],
            device_id=(freq, lax.rem(blk + step, 8)),
            device_id_type=MESH,
        )

    def group_step(group, carry):
        @pl.when(group == 0)
        def _():
            load(0).wait()

        @pl.when(group > 0)
        def _():
            load(group).wait()

        def filter_column(index, carry):
            weights = [jnp.broadcast_to(taps[pl.ds(t, 1), pl.ds(pl.multiple_of(index * LANES, LANES), LANES)], (16, LANES)) for t in range(TAPS)]
            for part in range(2):
                frames = []
                for frame in range(GROUP + TAPS - 1):
                    start = pl.multiple_of((group * GROUP + frame) * CH + index * LANES, LANES)
                    frames.append(volt[part, :, pl.ds(start, LANES)].astype(jnp.float32))
                for spec in range(GROUP):
                    total = weights[0] * frames[spec]
                    for tap in range(1, TAPS):
                        total = total + weights[tap] * frames[spec + tap]
                    filt[part, spec, index] = total.astype(jnp.bfloat16).astype(jnp.float32)
            return carry

        lax.fori_loop(0, COLS, filter_column, 0)

        for spec in range(GROUP):
            for half in range(2):
                rows_half = slice(half * 8, half * 8 + 8)
                values = []
                for index in range(COLS):
                    values.append(tuple(filt[part, spec, index, rows_half] for part in range(2)))
                for index, (real, imag) in enumerate(fft_columns(values)):
                    cos, sin = turn_cos[index], turn_sin[index]
                    place = pl.ds(half * LANES + spec * COLS + index, 8, stride=Z_STRIDE)
                    z_real[place, :] = real * cos - imag * sin
                    z_imag[place, :] = real * sin + imag * cos

        def last_step(block, carry):
            block_rows = pl.ds(pl.multiple_of(block * Z_STRIDE, 8), 256)
            both = jnp.concatenate([z_real[block_rows, :], z_imag[block_rows, :]], axis=1)
            high = both.astype(jnp.bfloat16)
            low = (both - high.astype(jnp.float32)).astype(jnp.bfloat16)
            total = lax.dot_general(dft_high[...], high, CONTRACT_LAST, preferred_element_type=jnp.float32)
            total = total + lax.dot_general(dft_low[...], high, CONTRACT_LAST, preferred_element_type=jnp.float32)
            total = total + lax.dot_general(dft_high[...], low, CONTRACT_LAST, preferred_element_type=jnp.float32)
            for part in range(2):
                for half in range(2):
                    piece = total[part * 128:part * 128 + 128, half * 128:half * 128 + 128]
                    wide[pl.ds(block * 4 + part * 2 + half, 128, stride=WIDE_STRIDE), :] = piece
            return carry

        lax.fori_loop(0, 8, last_step, 0, unroll=2)

        def narrow(index, carry):
            for sub in range(8):
                wide_rows = pl.ds(pl.multiple_of((index * 8 + sub) * WIDE_STRIDE, 8), 32)
                pieces[group, index * 8 + sub] = wide[wide_rows, :].astype(jnp.bfloat16)
            return carry

        lax.fori_loop(0, 16, narrow, 0)

        @pl.when(group == 0)
        def _():
            pl.semaphore_wait(barrier, 127)
            for step in range(1, 8):
                order_copy(step).start()

        def send(other_freq, other_side, other_col):
            pltpu.make_async_remote_copy(
                src_ref=pieces.at[group, other_freq * 8 + other_col * 2 + other_side],
                dst_ref=arrived.at[group, me],
                send_sem=send_sem.at[group],
                recv_sem=recv_sem.at[group],
                device_id=(other_freq, other_side * 4 + other_col),
                device_id_type=MESH,
            ).start()

        visit_others(send)
        pltpu.make_async_copy(pieces.at[group, freq * 8 + channel], arrived.at[group, me], own_sem.at[group]).start()
        return carry

    lax.fori_loop(0, GROUPS, group_step, 0)

    orders[blk] = own_order[...]
    for sem in range(2):
        pltpu.make_async_copy(orders.at[pl.ds(0, 7)], orders.at[pl.ds(0, 7)], order_sem.at[sem]).wait()
    members = lax.broadcasted_iota(jnp.int32, (256, 256), 0)
    for member in range(8):
        flags = (orders[member, 0:1, :] == members).astype(jnp.float32)
        chosen[member] = flags.T.astype(jnp.bfloat16)

    def take_group(group, carry):
        others = pl.ds(0, 127)
        pltpu.make_async_copy(pieces.at[group, freq * 8 + channel], arrived.at[group, me], own_sem.at[group]).wait()
        pltpu.make_async_copy(pieces.at[group, others], arrived.at[group, others], recv_sem.at[group]).wait()

        def unshuffle(index, carry):
            lanes = jnp.concatenate(
                [arrived[group, pl.ds(pl.multiple_of(index * 16 + step * 8, 8), 8)].reshape(256, LANES) for step in range(2)], axis=1
            )
            sorted_rows = jnp.dot(spread[...], lanes, preferred_element_type=jnp.float32).astype(jnp.bfloat16)
            for member in range(8):
                for part in range(2):
                    start = member * 32 + part * 16
                    for step in range(2):
                        place = pl.ds(pl.multiple_of(index * 32 + step * 16, 16), 16)
                        natural[member, place, part * LANES:part * LANES + LANES] = sorted_rows[start:start + 16, step * LANES:step * LANES + LANES]
            return carry

        lax.fori_loop(0, 8, unshuffle, 0, unroll=4)

        def arrange(member, carry):
            picked = jnp.dot(chosen[member], natural[member], preferred_element_type=jnp.float32).astype(jnp.bfloat16)
            for part in range(2):
                rows[member, part * GROUPS + group] = picked[:, part * LANES:part * LANES + LANES]
            return carry

        lax.fori_loop(0, 8, arrange, 0, unroll=4)
        return carry

    lax.fori_loop(0, GROUPS, take_group, 0)

    def side_of(member, part):
        return jnp.concatenate([rows[member, part * GROUPS + group] for group in range(GROUPS)], axis=1)

    def product(left, right):
        return lax.dot_general(left, right, CONTRACT_LAST, preferred_element_type=jnp.float32)

    def correlate(member, other):
        left_real, left_imag = side_of(member, 0), side_of(member, 1)
        right_real, right_imag = side_of(other, 0), side_of(other, 1)
        real = product(left_real, right_real) + product(left_imag, right_imag)
        imag = product(left_imag, right_real) - product(left_real, right_imag)
        return real * (1.0 / 512), imag * (1.0 / 512)

    def post(is_own, dest, source, place, send, receive, own):
        @pl.when(is_own)
        def _():
            pltpu.make_async_copy(source, place, own).start()

        @pl.when(jnp.logical_not(is_own))
        def _():
            pltpu.make_async_remote_copy(
                src_ref=source, dst_ref=place, send_sem=send, recv_sem=receive, device_id=(freq, dest), device_id_type=MESH
            ).start()

    def turn_target(turn):
        step = lax.rem(turn * 3 + 1, 8)
        return step, lax.rem(side + step // 4, 2) * 4 + lax.rem(col + lax.rem(step, 4), 4)

    def near_step(index, carry):
        lag = index // 8 + 1
        step, dest = turn_target(lax.rem(index, 8))
        values = correlate(dest, lax.rem(dest + lag, 8))
        for part in range(2):
            place = (lag - 1) * 2 + part
            tiles[dest, place] = values[part].astype(jnp.bfloat16)
            post(step == 0, dest, tiles.at[dest, place], near.at[channel, place], tile_sem.at[0], tile_sem.at[1], tile_sem.at[2])
        return carry

    lax.fori_loop(0, 24, near_step, 0)

    def packed_step(index, carry):
        step, dest = turn_target(index)
        real, imag = correlate(dest, dest)
        down = lax.broadcasted_iota(jnp.int32, (256, 256), 0)
        across = lax.broadcasted_iota(jnp.int32, (256, 256), 1)
        tiles[dest, 6] = jnp.where(down >= across, real, imag).astype(jnp.bfloat16)
        post(step == 0, dest, tiles.at[dest, 6], near.at[channel, 6], tile_sem.at[0], tile_sem.at[1], tile_sem.at[2])
        return carry

    lax.fori_loop(0, 8, packed_step, 0)

    def far_step(index, carry):
        step = lax.rem(index + 1, 4)
        dest = side * 4 + lax.rem(col + step, 4)
        values = correlate(dest, lax.rem(dest + 4, 8))
        for part in range(2):
            far_tiles[index, part] = values[part].astype(jnp.bfloat16)
            post(step == 0, dest, far_tiles.at[index, part], far.at[col, part], tile_sem.at[3], tile_sem.at[4], tile_sem.at[5])
        return carry

    lax.fori_loop(0, 4, far_step, 0)

    def finish(group, carry):
        others = pl.ds(0, 127)
        pltpu.make_async_copy(pieces.at[group, others], arrived.at[group, others], send_sem.at[group]).wait()
        return carry

    lax.fori_loop(0, GROUPS, finish, 0)
    pltpu.make_async_copy(tiles.at[0], near.at[0], tile_sem.at[2]).wait()
    for sem in (0, 1):
        pltpu.make_async_copy(tiles.at[pl.ds(0, 7)], near.at[pl.ds(0, 7)], tile_sem.at[sem]).wait()
    pltpu.make_async_copy(far_tiles.at[0], far.at[0], tile_sem.at[5]).wait()
    for sem in (3, 4):
        pltpu.make_async_copy(far_tiles.at[pl.ds(0, 3)], far.at[pl.ds(0, 3)], tile_sem.at[sem]).wait()


def tables():
    rows = np.arange(COLS)[:, None] * np.arange(LANES)[None, :]
    angles = -2.0 * np.pi * rows / CH
    steps = np.arange(LANES)
    turn = -2.0 * np.pi * (steps[:, None] * steps[None, :] % LANES) / LANES
    dft = np.block([[np.cos(turn), -np.sin(turn)], [np.sin(turn), np.cos(turn)]])
    parts = [np.cos(angles) / 64, np.sin(angles) / 64, dft[:, :LANES], dft[:, LANES:]]
    return jnp.asarray(np.concatenate(parts, axis=0), jnp.float32)


def make_tiles(voltages, pfb_taps, order_table):
    anywhere = pl.BlockSpec(memory_space=pl.ANY)
    return pl.pallas_call(
        correlator_kernel,
        out_shape=(
            jax.ShapeDtypeStruct((8, 7, 256, 256), jnp.bfloat16),
            jax.ShapeDtypeStruct((4, 2, 256, 256), jnp.bfloat16),
        ),
        in_specs=[anywhere] + [pl.BlockSpec(memory_space=pltpu.VMEM)] * 3,
        out_specs=(anywhere, anywhere),
        scratch_shapes=[pltpu.VMEM(voltages.shape, jnp.bfloat16)]
        + [
            pltpu.VMEM((COLS, 8, LANES), jnp.float32),
            pltpu.VMEM((COLS, 8, LANES), jnp.float32),
            pltpu.VMEM((256, 256), jnp.bfloat16),
            pltpu.VMEM((256, 256), jnp.bfloat16),
            pltpu.VMEM((256, 256), jnp.bfloat16),
            pltpu.VMEM((2, GROUP, COLS, 16, LANES), jnp.float32),
            pltpu.VMEM((8 * Z_STRIDE, LANES), jnp.float32),
            pltpu.VMEM((8 * Z_STRIDE, LANES), jnp.float32),
            pltpu.VMEM((128 * WIDE_STRIDE, LANES), jnp.float32),
            pltpu.VMEM((GROUPS, 128, 32, LANES), jnp.bfloat16),
            pltpu.VMEM((GROUPS, 128, 32, LANES), jnp.bfloat16),
            pltpu.VMEM((8, 256), jnp.int32),
            pltpu.VMEM((8, 8, 256), jnp.int32),
            pltpu.VMEM((8, 256, 256), jnp.bfloat16),
            pltpu.VMEM((8, 256, 256), jnp.bfloat16),
            pltpu.VMEM((8, 8, 256, LANES), jnp.bfloat16),
            pltpu.VMEM((8, 7, 256, 256), jnp.bfloat16),
            pltpu.VMEM((4, 2, 256, 256), jnp.bfloat16),
            pltpu.SemaphoreType.DMA((GROUPS,)),
            pltpu.SemaphoreType.DMA((GROUPS,)),
            pltpu.SemaphoreType.DMA((GROUPS,)),
            pltpu.SemaphoreType.DMA((GROUPS,)),
            pltpu.SemaphoreType.DMA((2,)),
            pltpu.SemaphoreType.DMA((6,)),
        ],
        compiler_params=pltpu.CompilerParams(vmem_limit_bytes=42 * 2**20, collective_id=0, has_side_effects=True),
        cost_estimate=pl.CostEstimate(flops=10**10, bytes_accessed=16 * 2**20, transcendentals=0),
    )(voltages, order_table, pfb_taps, tables())


def arrange_kernel(lag_table, near, far, visibility, far_visibility, unpacked, sems):
    far_copy = pltpu.make_async_copy(far, far_visibility.at[:, 0], sems.at[0])
    far_copy.start()
    for slot in range(4):
        lag = lag_table[slot]

        @pl.when(lag > 0)
        def _(slot=slot, lag=lag):
            pltpu.make_async_copy(near.at[:, pl.ds((lag - 1) * 2, 2)], visibility.at[:, 0, slot], sems.at[1]).start()

    own_slot = 0
    for slot in range(4):
        own_slot = jnp.where(lag_table[slot] == 0, slot, own_slot)
    down = lax.broadcasted_iota(jnp.int32, (256, 256), 0)
    across = lax.broadcasted_iota(jnp.int32, (256, 256), 1)

    def unpack(out, carry):
        packed = near[out, 6].astype(jnp.float32)
        turned = packed.T
        unpacked[out, 0] = jnp.where(down >= across, packed, turned).astype(jnp.bfloat16)
        mirrored = jnp.where(down > across, -turned, 0.0)
        unpacked[out, 1] = jnp.where(down < across, packed, mirrored).astype(jnp.bfloat16)
        pltpu.make_async_copy(unpacked.at[out], visibility.at[out, 0, own_slot], sems.at[2]).start()
        return carry

    lax.fori_loop(0, 8, unpack, 0)
    far_copy.wait()
    for slot in range(4):
        @pl.when(lag_table[slot] > 0)
        def _(slot=slot):
            pltpu.make_async_copy(near.at[:, pl.ds(0, 2)], visibility.at[:, 0, slot], sems.at[1]).wait()

    pltpu.make_async_copy(unpacked, visibility.at[:, 0, 0], sems.at[2]).wait()


def arrange(near, far, lag_table):
    return pl.pallas_call(
        arrange_kernel,
        out_shape=(
            jax.ShapeDtypeStruct((8, 1, 4, 2, 256, 256), jnp.bfloat16),
            jax.ShapeDtypeStruct((4, 1, 2, 256, 256), jnp.bfloat16),
        ),
        in_specs=[pl.BlockSpec(memory_space=pltpu.SMEM), pl.BlockSpec(memory_space=pltpu.VMEM), pl.BlockSpec(memory_space=pltpu.VMEM)],
        out_specs=(pl.BlockSpec(memory_space=pl.ANY), pl.BlockSpec(memory_space=pl.ANY)),
        scratch_shapes=[pltpu.VMEM((8, 2, 256, 256), jnp.bfloat16), pltpu.SemaphoreType.DMA((3,))],
        compiler_params=pltpu.CompilerParams(vmem_limit_bytes=16 * 2**20),
    )(lag_table, near, far)


def per_device(voltages, pfb_taps, order_table, lag_table):
    near, far = make_tiles(voltages, pfb_taps, order_table)
    return arrange(near, far, lag_table)


def solution(mesh):
    placed = (P(None, ("freq", "blk"), None), P(), P("blk", None), P())
    return jax.shard_map(
        per_device,
        mesh=mesh,
        in_specs=placed,
        out_specs=(P("freq", "blk", None, None, None, None), P("freq", "blk", None, None, None)),
        check_vma=False,
    )
```

```python
import functools
import math

import jax
import jax.numpy as jnp
import numpy as np
from jax import lax
from jax.experimental import pallas as pl
from jax.experimental.pallas import tpu as pltpu
from jax.sharding import PartitionSpec as P

CH = 4096
TAPS = 16
SPECTRA = 16
COLS = 32
LANES = 128
GROUP = 4
GROUPS = 4
WHOLE_GROUPS = 1
Z_STRIDE = 264
WIDE_STRIDE = 40


def complex_mul(value, turn):
    real, imag = value
    cos, sin = float(turn.real), float(turn.imag)
    if abs(sin) < 1e-12 and abs(cos - 1) < 1e-12:
        return value
    if abs(cos) < 1e-12 and abs(sin + 1) < 1e-12:
        return (imag, -real)
    if abs(cos + sin) < 1e-12:
        return ((real + imag) * cos, (imag - real) * cos)
    if abs(cos - sin) < 1e-12:
        return ((real - imag) * cos, (real + imag) * cos)
    return (real * cos - imag * sin, real * sin + imag * cos)


def fft_list(values):
    count = len(values)
    if count == 1:
        return values
    if count == 2:
        (ar, ai), (br, bi) = values
        return [(ar + br, ai + bi), (ar - br, ai - bi)]
    if count == 4:
        even = fft_list([values[0], values[2]])
        odd = fft_list([values[1], values[3]])
    else:
        even = fft_list(values[0::2])
        odd = fft_list(values[1::2])
    half = count // 2
    low, high = [], []
    for index in range(half):
        turned = complex_mul(odd[index], np.exp(-2j * np.pi * index / count))
        base = even[index]
        low.append((base[0] + turned[0], base[1] + turned[1]))
        high.append((base[0] - turned[0], base[1] - turned[1]))
    return low + high


def fft_columns(values):
    sections = []
    for low in range(8):
        parts = fft_list([values[8 * high + low] for high in range(4)])
        sections.append([complex_mul(part, np.exp(-2j * np.pi * low * index / 32)) for index, part in enumerate(parts)])
    result = [None] * 32
    for index in range(4):
        parts = fft_list([sections[low][index] for low in range(8)])
        for high in range(8):
            result[index + 4 * high] = parts[high]
    return result


MESH = pl.DeviceIdType.MESH
CONTRACT_LAST = (((1,), (1,)), ((), ()))


def position():
    freq = lax.axis_index("freq")
    blk = lax.axis_index("blk")
    return (lax.rem(blk, 4), lax.rem(freq // 2, 2) * 2 + blk // 4, freq // 4, lax.rem(freq, 2))


def mesh_ids(col, row, layer, core):
    return (layer * 4 + (row // 2) * 2 + core, lax.rem(row, 2) * 4 + col)


def correlator_kernel(
    volt_far, order_row, taps, numbers,
    near, mirror, far,
    volt, turn_cos, turn_sin, dft_high, dft_low, spread,
    filt, z_real, z_imag, wide, pieces, arrived, own_order, orders, chosen, natural, rows, tiles, far_tiles, packed, unpacked,
    load_sem, send_sem, recv_sem, own_sem, order_sem, tile_sem,
):
    def load(group):
        first = 0 if isinstance(group, int) else pl.multiple_of((group * GROUP + TAPS - 1) * CH, LANES)
        size = (GROUP + TAPS - 1) * CH if isinstance(group, int) else GROUP * CH
        place = (slice(None), slice(None), pl.ds(first, size))
        return pltpu.make_async_copy(volt_far.at[place], volt.at[place], load_sem.at[group])

    load(0).start()
    for later in range(1, GROUPS):
        load(jnp.int32(later)).start()

    col, row, layer, core = position()
    freq, blk = mesh_ids(col, row, layer, core)
    me = freq * 8 + blk
    side = blk // 4
    channel = col * 2 + side

    def visit_others(visit):
        cols = [lax.rem(col + step, 4) for step in range(4)]

        def visit_plane(index, carry):
            new_row = lax.rem(row + lax.rem(index, 4), 4)
            new_layer = lax.rem(layer + lax.rem(lax.div(index, 4), 4), 4)
            new_core = lax.rem(core + lax.div(index, 16), 2)
            other_freq = new_layer * 4 + lax.div(new_row, 2) * 2 + new_core
            other_side = lax.rem(new_row, 2)

            @pl.when(index > 0)
            def _():
                visit(other_freq, other_side, cols[0])

            for step in range(1, 4):
                visit(other_freq, other_side, cols[step])
            return carry

        lax.fori_loop(0, 32, visit_plane, 0)

    barrier = pltpu.get_barrier_semaphore()

    def greet(other_freq, other_side, other_col):
        pl.semaphore_signal(barrier, inc=1, device_id=(other_freq, other_side * 4 + other_col), device_id_type=MESH)

    visit_others(greet)
    own_order[...] = jnp.broadcast_to(order_row[...], (8, 256))
    for index in range(COLS):
        turn_cos[index] = jnp.broadcast_to(numbers[index:index + 1, :], (8, LANES))
        turn_sin[index] = jnp.broadcast_to(numbers[COLS + index:COLS + index + 1, :], (8, LANES))
    dft = jnp.concatenate([numbers[2 * COLS:2 * COLS + 256, :], numbers[2 * COLS + 256:2 * COLS + 512, :]], axis=1)
    dft_high[...] = dft.astype(jnp.bfloat16)
    dft_low[...] = (dft - dft.astype(jnp.bfloat16).astype(jnp.float32)).astype(jnp.bfloat16)
    sorted_row = lax.broadcasted_iota(jnp.int32, (256, 256), 0)
    came_row = lax.broadcasted_iota(jnp.int32, (256, 256), 1)
    wanted = jnp.bitwise_and(sorted_row, 30) * 8 + lax.shift_right_logical(sorted_row, 5) * 2 + jnp.bitwise_and(sorted_row, 1)
    spread[...] = (wanted == came_row).astype(jnp.float32).astype(jnp.bfloat16)

    def order_copy(step):
        return pltpu.make_async_remote_copy(
            src_ref=own_order,
            dst_ref=orders.at[blk],
            send_sem=order_sem.at[0],
            recv_sem=order_sem.at[1],
            device_id=(freq, lax.rem(blk + step, 8)),
            device_id_type=MESH,
        )

    def half_rows(half):
        return pl.ds(pl.multiple_of(half * 16, 16), 16)

    first = lax.rem(side + core, 2)
    second = 1 - first

    def send_piece(group, part, half, other_freq, other_side, other_col):
        pltpu.make_async_remote_copy(
            src_ref=pieces.at[group, other_freq * 8 + other_col * 2 + other_side, part],
            dst_ref=arrived.at[group, me, part],
            send_sem=send_sem.at[half, group],
            recv_sem=recv_sem.at[half, group],
            device_id=(other_freq, other_side * 4 + other_col),
            device_id_type=MESH,
        ).start()

    def own_piece(group):
        return pltpu.make_async_copy(pieces.at[group, freq * 8 + channel], arrived.at[group, me], own_sem.at[group])

    def wait_pieces(group, part, half, sems):
        place = (group, pl.ds(0, 127), part)
        pltpu.make_async_copy(pieces.at[place], arrived.at[place], sems.at[half, group]).wait()

    def group_step(group, carry):
        @pl.when(group == 0)
        def _():
            load(0).wait()

        @pl.when(group > 0)
        def _():
            load(group).wait()

        def filter_column(index, carry):
            weights = [jnp.broadcast_to(taps[pl.ds(t, 1), pl.ds(pl.multiple_of(index * LANES, LANES), LANES)], (16, LANES)) for t in range(TAPS)]
            for part in range(2):
                frames = []
                for frame in range(GROUP + TAPS - 1):
                    start = pl.multiple_of((group * GROUP + frame) * CH + index * LANES, LANES)
                    frames.append(volt[part, :, pl.ds(start, LANES)].astype(jnp.float32))
                for spec in range(GROUP):
                    total = weights[0] * frames[spec]
                    for tap in range(1, TAPS):
                        total = total + weights[tap] * frames[spec + tap]
                    filt[part, spec, index] = total.astype(jnp.bfloat16).astype(jnp.float32)
            return carry

        lax.fori_loop(0, COLS, filter_column, 0)

        for spec in range(GROUP):
            for half in range(2):
                rows_half = slice(half * 8, half * 8 + 8)
                values = []
                for index in range(COLS):
                    values.append(tuple(filt[part, spec, index, rows_half] for part in range(2)))
                for index, (real, imag) in enumerate(fft_columns(values)):
                    cos, sin = turn_cos[index], turn_sin[index]
                    place = pl.ds(half * LANES + spec * COLS + index, 8, stride=Z_STRIDE)
                    z_real[place, :] = real * cos - imag * sin
                    z_imag[place, :] = real * sin + imag * cos

        def last_step(block, carry):
            block_rows = pl.ds(pl.multiple_of(block * Z_STRIDE, 8), 256)
            both = jnp.concatenate([z_real[block_rows, :], z_imag[block_rows, :]], axis=1)
            high = both.astype(jnp.bfloat16)
            low = (both - high.astype(jnp.float32)).astype(jnp.bfloat16)
            total = lax.dot_general(dft_high[...], high, CONTRACT_LAST, preferred_element_type=jnp.float32)
            total = total + lax.dot_general(dft_low[...], high, CONTRACT_LAST, preferred_element_type=jnp.float32)
            total = total + lax.dot_general(dft_high[...], low, CONTRACT_LAST, preferred_element_type=jnp.float32)
            for part in range(2):
                for half in range(2):
                    piece = total[part * 128:part * 128 + 128, half * 128:half * 128 + 128]
                    wide[pl.ds(block * 4 + part * 2 + half, 128, stride=WIDE_STRIDE), :] = piece
            return carry

        lax.fori_loop(0, 8, last_step, 0, unroll=2)

        def narrow(index, carry):
            for sub in range(8):
                wide_rows = pl.ds(pl.multiple_of((index * 8 + sub) * WIDE_STRIDE, 8), 32)
                pieces[group, index * 8 + sub] = wide[wide_rows, :].astype(jnp.bfloat16)
            return carry

        lax.fori_loop(0, 16, narrow, 0)

        @pl.when(group == 0)
        def _():
            pl.semaphore_wait(barrier, 127)
            for step in range(1, 8):
                order_copy(step).start()

        @pl.when(group < WHOLE_GROUPS)
        def _():
            def send(other_freq, other_side, other_col):
                send_piece(group, slice(None), 0, other_freq, other_side, other_col)

            visit_others(send)

        @pl.when(group >= WHOLE_GROUPS)
        def _():
            def send(other_freq, other_side, other_col):
                send_piece(group, half_rows(lax.rem(other_side + lax.rem(other_freq, 2), 2)), 0, other_freq, other_side, other_col)

            visit_others(send)

        own_piece(group).start()
        return carry

    lax.fori_loop(0, GROUPS, group_step, 0)

    def send_rest(group, carry):
        def send(other_freq, other_side, other_col):
            send_piece(group, half_rows(lax.rem(1 + other_side + lax.rem(other_freq, 2), 2)), 1, other_freq, other_side, other_col)

        visit_others(send)
        return carry

    lax.fori_loop(WHOLE_GROUPS, GROUPS, send_rest, 0)

    orders[blk] = own_order[...]
    for sem in range(2):
        pltpu.make_async_copy(orders.at[pl.ds(0, 7)], orders.at[pl.ds(0, 7)], order_sem.at[sem]).wait()
    members = lax.broadcasted_iota(jnp.int32, (256, 256), 0)
    for member in range(8):
        flags = (orders[member, 0:1, :] == members).astype(jnp.float32)
        chosen[member] = flags.T.astype(jnp.bfloat16)

    def take_half(group, half):
        def unshuffle(index, carry):
            lanes = jnp.concatenate(
                [
                    arrived[group, pl.ds(pl.multiple_of(index * 32 + step * 16, 16), 16), half_rows(half)].reshape(256, LANES)
                    for step in range(2)
                ],
                axis=1,
            )
            sorted_rows = jnp.dot(spread[...], lanes, preferred_element_type=jnp.float32).astype(jnp.bfloat16)
            for member in range(4):
                for part in range(2):
                    start = member * 64 + part * 32
                    for step in range(2):
                        place = pl.ds(pl.multiple_of(index * 64 + step * 32, 32), 32)
                        natural[half * 4 + member, place, part * LANES:part * LANES + LANES] = sorted_rows[start:start + 32, step * LANES:step * LANES + LANES]
            return carry

        lax.fori_loop(0, 4, unshuffle, 0, unroll=4)

        def arrange(index, carry):
            member = half * 4 + index
            picked = jnp.dot(chosen[member], natural[member], preferred_element_type=jnp.float32).astype(jnp.bfloat16)
            for part in range(2):
                rows[member, part * GROUPS + group] = picked[:, part * LANES:part * LANES + LANES]
            return carry

        lax.fori_loop(0, 4, arrange, 0, unroll=4)

    def take_whole(group, carry):
        own_piece(group).wait()
        wait_pieces(group, slice(None), 0, recv_sem)
        for half in range(2):
            take_half(group, half)
        return carry

    lax.fori_loop(0, WHOLE_GROUPS, take_whole, 0)

    def take_first(group, carry):
        own_piece(group).wait()
        wait_pieces(group, pl.ds(0, 16), 0, recv_sem)
        take_half(group, first)
        return carry

    lax.fori_loop(WHOLE_GROUPS, GROUPS, take_first, 0)

    def side_of(member, part):
        return jnp.concatenate([rows[member, part * GROUPS + group] for group in range(GROUPS)], axis=1)

    def product(left, right):
        return lax.dot_general(left, right, CONTRACT_LAST, preferred_element_type=jnp.float32)

    def correlate(member, other):
        left_real, left_imag = side_of(member, 0), side_of(member, 1)
        right_real, right_imag = side_of(other, 0), side_of(other, 1)
        real = product(left_real, right_real) + product(left_imag, right_imag)
        imag = product(left_imag, right_real) - product(left_real, right_imag)
        return real * (1.0 / 512), imag * (1.0 / 512)

    def post(is_own, dest, source, place, send, receive, own):
        @pl.when(is_own)
        def _():
            pltpu.make_async_copy(source, place, own).start()

        @pl.when(jnp.logical_not(is_own))
        def _():
            pltpu.make_async_remote_copy(
                src_ref=source, dst_ref=place, send_sem=send, recv_sem=receive, device_id=(freq, dest), device_id_type=MESH
            ).start()

    def turn_target(turn):
        step = lax.rem(turn * 3 + 1, 8)
        return step, lax.rem(side + step // 4, 2) * 4 + lax.rem(col + lax.rem(step, 4), 4)

    def send_near(is_own, dest, lag):
        values = correlate(dest, lax.rem(dest + lag, 8))
        for part in range(2):
            place = (lag - 1) * 2 + part
            tiles[dest, place] = values[part].astype(jnp.bfloat16)
            post(is_own, dest, tiles.at[dest, place], near.at[channel, place], tile_sem.at[0], tile_sem.at[1], tile_sem.at[2])

    def send_packed(is_own, dest):
        real, imag = correlate(dest, dest)
        down = lax.broadcasted_iota(jnp.int32, (256, 256), 0)
        across = lax.broadcasted_iota(jnp.int32, (256, 256), 1)
        tiles[dest, 6] = jnp.where(down >= across, real, imag).astype(jnp.bfloat16)
        post(is_own, dest, tiles.at[dest, 6], packed.at[channel], tile_sem.at[6], tile_sem.at[7], tile_sem.at[8])

    def early_packed(index, carry):
        dest = first * 4 + lax.rem(col + index + 1, 4)
        send_packed(dest == blk, dest)
        return carry

    lax.fori_loop(0, 4, early_packed, 0)

    def early_near(index, carry):
        lag = lax.div(index, 4) + 1
        dest_col = lax.rem(col + lax.rem(index, 4) + 1, 4)
        dest = first * 4 + dest_col

        @pl.when(dest_col + lag < 4)
        def _():
            send_near(dest == blk, dest, lag)

        return carry

    lax.fori_loop(0, 12, early_near, 0)

    def take_second(group, carry):
        wait_pieces(group, pl.ds(16, 16), 1, recv_sem)
        take_half(group, second)
        return carry

    lax.fori_loop(WHOLE_GROUPS, GROUPS, take_second, 0)

    def near_step(index, carry):
        lag = lax.div(index, 8) + 1
        step, dest = turn_target(lax.rem(index, 8))

        @pl.when(jnp.logical_or(lax.div(dest, 4) != first, lax.rem(dest, 4) + lag >= 4))
        def _():
            send_near(step == 0, dest, lag)

        return carry

    def late_packed(index, carry):
        dest = second * 4 + lax.rem(col + index + 1, 4)
        send_packed(dest == blk, dest)
        return carry

    lax.fori_loop(0, 4, late_packed, 0)
    lax.fori_loop(0, 24, near_step, 0)

    def far_step(index, carry):
        step = lax.rem(index + 1, 4)
        dest = side * 4 + lax.rem(col + step, 4)
        values = correlate(dest, lax.rem(dest + 4, 8))
        for part in range(2):
            far_tiles[index, part] = values[part].astype(jnp.bfloat16)
            post(step == 0, dest, far_tiles.at[index, part], far.at[col, part], tile_sem.at[3], tile_sem.at[4], tile_sem.at[5])
        return carry

    lax.fori_loop(0, 4, far_step, 0)

    def finish_whole(group, carry):
        wait_pieces(group, slice(None), 0, send_sem)
        return carry

    def finish_halves(group, carry):
        for half in range(2):
            wait_pieces(group, pl.ds(half * 16, 16), half, send_sem)
        return carry

    lax.fori_loop(0, WHOLE_GROUPS, finish_whole, 0)
    lax.fori_loop(WHOLE_GROUPS, GROUPS, finish_halves, 0)

    pltpu.make_async_copy(tiles.at[0, 6], packed.at[0], tile_sem.at[8]).wait()
    for sem in (6, 7):
        pltpu.make_async_copy(packed.at[pl.ds(0, 7)], packed.at[pl.ds(0, 7)], tile_sem.at[sem]).wait()

    def unpack(index, carry):
        triangles = packed[index].astype(jnp.float32)
        turned = triangles.T
        down = lax.broadcasted_iota(jnp.int32, (256, 256), 0)
        across = lax.broadcasted_iota(jnp.int32, (256, 256), 1)
        unpacked[index, 0] = jnp.where(down >= across, triangles, turned).astype(jnp.bfloat16)
        mirrored = jnp.where(down > across, -turned, 0.0)
        unpacked[index, 1] = jnp.where(down < across, triangles, mirrored).astype(jnp.bfloat16)
        return carry

    lax.fori_loop(0, 8, unpack, 0)
    unpacked_copy = pltpu.make_async_copy(unpacked, mirror, tile_sem.at[9])
    unpacked_copy.start()
    unpacked_copy.wait()

    whole_parts = pl.ds(0, 6)
    pltpu.make_async_copy(tiles.at[0, whole_parts], near.at[0, whole_parts], tile_sem.at[2]).wait()
    for sem in (0, 1):
        pltpu.make_async_copy(tiles.at[pl.ds(0, 7), whole_parts], near.at[pl.ds(0, 7), whole_parts], tile_sem.at[sem]).wait()
    pltpu.make_async_copy(far_tiles.at[0], far.at[0], tile_sem.at[5]).wait()
    for sem in (3, 4):
        pltpu.make_async_copy(far_tiles.at[pl.ds(0, 3)], far.at[pl.ds(0, 3)], tile_sem.at[sem]).wait()


def tables():
    rows = np.arange(COLS)[:, None] * np.arange(LANES)[None, :]
    angles = -2.0 * np.pi * rows / CH
    steps = np.arange(LANES)
    turn = -2.0 * np.pi * (steps[:, None] * steps[None, :] % LANES) / LANES
    dft = np.block([[np.cos(turn), -np.sin(turn)], [np.sin(turn), np.cos(turn)]])
    parts = [np.cos(angles) / 64, np.sin(angles) / 64, dft[:, :LANES], dft[:, LANES:]]
    return jnp.asarray(np.concatenate(parts, axis=0), jnp.float32)


def make_tiles(voltages, pfb_taps, order_table):
    anywhere = pl.BlockSpec(memory_space=pl.ANY)
    return pl.pallas_call(
        correlator_kernel,
        out_shape=(
            jax.ShapeDtypeStruct((8, 6, 256, 256), jnp.bfloat16),
            jax.ShapeDtypeStruct((8, 2, 256, 256), jnp.bfloat16),
            jax.ShapeDtypeStruct((4, 2, 256, 256), jnp.bfloat16),
        ),
        in_specs=[anywhere] + [pl.BlockSpec(memory_space=pltpu.VMEM)] * 3,
        out_specs=(anywhere, anywhere, anywhere),
        scratch_shapes=[pltpu.VMEM(voltages.shape, jnp.bfloat16)]
        + [
            pltpu.VMEM((COLS, 8, LANES), jnp.float32),
            pltpu.VMEM((COLS, 8, LANES), jnp.float32),
            pltpu.VMEM((256, 256), jnp.bfloat16),
            pltpu.VMEM((256, 256), jnp.bfloat16),
            pltpu.VMEM((256, 256), jnp.bfloat16),
            pltpu.VMEM((2, GROUP, COLS, 16, LANES), jnp.float32),
            pltpu.VMEM((8 * Z_STRIDE, LANES), jnp.float32),
            pltpu.VMEM((8 * Z_STRIDE, LANES), jnp.float32),
            pltpu.VMEM((128 * WIDE_STRIDE, LANES), jnp.float32),
            pltpu.VMEM((GROUPS, 128, 32, LANES), jnp.bfloat16),
            pltpu.VMEM((GROUPS, 128, 32, LANES), jnp.bfloat16),
            pltpu.VMEM((8, 256), jnp.int32),
            pltpu.VMEM((8, 8, 256), jnp.int32),
            pltpu.VMEM((8, 256, 256), jnp.bfloat16),
            pltpu.VMEM((8, 256, 256), jnp.bfloat16),
            pltpu.VMEM((8, 8, 256, LANES), jnp.bfloat16),
            pltpu.VMEM((8, 7, 256, 256), jnp.bfloat16),
            pltpu.VMEM((4, 2, 256, 256), jnp.bfloat16),
            pltpu.VMEM((8, 256, 256), jnp.bfloat16),
            pltpu.VMEM((8, 2, 256, 256), jnp.bfloat16),
            pltpu.SemaphoreType.DMA((GROUPS,)),
            pltpu.SemaphoreType.DMA((2, GROUPS)),
            pltpu.SemaphoreType.DMA((2, GROUPS)),
            pltpu.SemaphoreType.DMA((GROUPS,)),
            pltpu.SemaphoreType.DMA((2,)),
            pltpu.SemaphoreType.DMA((10,)),
        ],
        compiler_params=pltpu.CompilerParams(vmem_limit_bytes=44 * 2**20, collective_id=0, has_side_effects=True),
        cost_estimate=pl.CostEstimate(flops=10**10, bytes_accessed=16 * 2**20, transcendentals=0),
    )(voltages, order_table, pfb_taps, tables())


def arrange_kernel(lag_table, near, mirror, far, visibility, far_visibility, sems):
    far_copy = pltpu.make_async_copy(far, far_visibility.at[:, 0], sems.at[0])
    far_copy.start()
    for slot in range(4):
        lag = lag_table[slot]

        @pl.when(lag == 0)
        def _(slot=slot):
            for out in range(8):
                pltpu.make_async_copy(mirror.at[out], visibility.at[out, 0, slot], sems.at[slot + 1]).start()

        @pl.when(lag > 0)
        def _(slot=slot, lag=lag):
            for out in range(8):
                pltpu.make_async_copy(near.at[out, pl.ds((lag - 1) * 2, 2)], visibility.at[out, 0, slot], sems.at[slot + 1]).start()

    for slot in range(4):
        pltpu.make_async_copy(mirror, visibility.at[:, 0, slot], sems.at[slot + 1]).wait()
    far_copy.wait()


def arrange(near, mirror, far, lag_table):
    return pl.pallas_call(
        arrange_kernel,
        out_shape=(
            jax.ShapeDtypeStruct((8, 1, 4, 2, 256, 256), jnp.bfloat16),
            jax.ShapeDtypeStruct((4, 1, 2, 256, 256), jnp.bfloat16),
        ),
        in_specs=[pl.BlockSpec(memory_space=pltpu.SMEM)] + [pl.BlockSpec(memory_space=pltpu.VMEM)] * 3,
        out_specs=(pl.BlockSpec(memory_space=pl.ANY), pl.BlockSpec(memory_space=pl.ANY)),
        scratch_shapes=[pltpu.SemaphoreType.DMA((5,))],
        compiler_params=pltpu.CompilerParams(vmem_limit_bytes=2**20),
    )(lag_table, near, mirror, far)


def per_device(voltages, pfb_taps, order_table, lag_table):
    near, mirror, far = make_tiles(voltages, pfb_taps, order_table)
    return arrange(near, mirror, far, lag_table)


def solution(mesh):
    placed = (P(None, ("freq", "blk"), None), P(), P("blk", None), P())
    return jax.shard_map(
        per_device,
        mesh=mesh,
        in_specs=placed,
        out_specs=(P("freq", "blk", None, None, None, None), P("freq", "blk", None, None, None)),
        check_vma=False,
    )
```

```python
import functools
import math

import jax
import jax.numpy as jnp
import numpy as np
from jax import lax
from jax.experimental import pallas as pl
from jax.experimental.pallas import tpu as pltpu
from jax.sharding import PartitionSpec as P

CH = 4096
TAPS = 16
SPECTRA = 16
COLS = 32
LANES = 128
GROUP = 4
GROUPS = 4
WHOLE_GROUPS = 1
Z_STRIDE = 264
WIDE_STRIDE = 40


def complex_mul(value, turn):
    real, imag = value
    cos, sin = float(turn.real), float(turn.imag)
    if abs(sin) < 1e-12 and abs(cos - 1) < 1e-12:
        return value
    if abs(cos) < 1e-12 and abs(sin + 1) < 1e-12:
        return (imag, -real)
    if abs(cos + sin) < 1e-12:
        return ((real + imag) * cos, (imag - real) * cos)
    if abs(cos - sin) < 1e-12:
        return ((real - imag) * cos, (real + imag) * cos)
    return (real * cos - imag * sin, real * sin + imag * cos)


def fft_list(values):
    count = len(values)
    if count == 1:
        return values
    if count == 2:
        (ar, ai), (br, bi) = values
        return [(ar + br, ai + bi), (ar - br, ai - bi)]
    if count == 4:
        even = fft_list([values[0], values[2]])
        odd = fft_list([values[1], values[3]])
    else:
        even = fft_list(values[0::2])
        odd = fft_list(values[1::2])
    half = count // 2
    low, high = [], []
    for index in range(half):
        turned = complex_mul(odd[index], np.exp(-2j * np.pi * index / count))
        base = even[index]
        low.append((base[0] + turned[0], base[1] + turned[1]))
        high.append((base[0] - turned[0], base[1] - turned[1]))
    return low + high


def fft_columns(values):
    sections = []
    for low in range(8):
        parts = fft_list([values[8 * high + low] for high in range(4)])
        sections.append([complex_mul(part, np.exp(-2j * np.pi * low * index / 32)) for index, part in enumerate(parts)])
    result = [None] * 32
    for index in range(4):
        parts = fft_list([sections[low][index] for low in range(8)])
        for high in range(8):
            result[index + 4 * high] = parts[high]
    return result


MESH = pl.DeviceIdType.MESH
CONTRACT_LAST = (((1,), (1,)), ((), ()))


def position():
    freq = lax.axis_index("freq")
    blk = lax.axis_index("blk")
    return (lax.rem(blk, 4), lax.rem(freq // 2, 2) * 2 + blk // 4, freq // 4, lax.rem(freq, 2))


def mesh_ids(col, row, layer, core):
    return (layer * 4 + (row // 2) * 2 + core, lax.rem(row, 2) * 4 + col)


def unit_circle(steps, count):
    centered = jnp.where(steps > count // 2, steps - count, steps).astype(jnp.float32)
    angle = centered * (2 * math.pi / count)
    square = angle * angle
    cos = jnp.zeros_like(angle)
    sin = jnp.zeros_like(angle)
    for order in range(9, -1, -1):
        cos = cos * square + (-1) ** order / math.factorial(2 * order)
        sin = sin * square + (-1) ** order / math.factorial(2 * order + 1)
    return cos, sin * angle


def correlator_kernel(
    volt_far, order_row, taps,
    near, mirror, far,
    volt, turn_cos, turn_sin, dft_high, dft_low, spread,
    filt, z_real, z_imag, wide, pieces, arrived, own_order, orders, chosen, natural, rows, tiles, far_tiles, packed, unpacked,
    load_sem, send_sem, recv_sem, own_sem, order_sem, tile_sem,
):
    def load(group):
        first = 0 if isinstance(group, int) else pl.multiple_of((group * GROUP + TAPS - 1) * CH, LANES)
        size = (GROUP + TAPS - 1) * CH if isinstance(group, int) else GROUP * CH
        place = (slice(None), slice(None), pl.ds(first, size))
        return pltpu.make_async_copy(volt_far.at[place], volt.at[place], load_sem.at[group])

    load(0).start()
    for later in range(1, GROUPS):
        load(jnp.int32(later)).start()

    col, row, layer, core = position()
    freq, blk = mesh_ids(col, row, layer, core)
    me = freq * 8 + blk
    side = blk // 4
    channel = col * 2 + side

    def visit_others(visit):
        cols = [lax.rem(col + step, 4) for step in range(4)]

        def visit_plane(index, carry):
            new_row = lax.rem(row + lax.rem(index, 4), 4)
            new_layer = lax.rem(layer + lax.rem(lax.div(index, 4), 4), 4)
            new_core = lax.rem(core + lax.div(index, 16), 2)
            other_freq = new_layer * 4 + lax.div(new_row, 2) * 2 + new_core
            other_side = lax.rem(new_row, 2)

            @pl.when(index > 0)
            def _():
                visit(other_freq, other_side, cols[0])

            for step in range(1, 4):
                visit(other_freq, other_side, cols[step])
            return carry

        lax.fori_loop(0, 32, visit_plane, 0)

    barrier = pltpu.get_barrier_semaphore()

    def greet(other_freq, other_side, other_col):
        pl.semaphore_signal(barrier, inc=1, device_id=(other_freq, other_side * 4 + other_col), device_id_type=MESH)

    visit_others(greet)
    own_order[...] = jnp.broadcast_to(order_row[...], (8, 256))
    fine = lax.broadcasted_iota(jnp.int32, (COLS, LANES), 0) * lax.broadcasted_iota(jnp.int32, (COLS, LANES), 1)
    fine_cos, fine_sin = unit_circle(fine, CH)
    for index in range(COLS):
        turn_cos[index] = jnp.broadcast_to(fine_cos[index:index + 1, :] * (1.0 / 64), (8, LANES))
        turn_sin[index] = jnp.broadcast_to(fine_sin[index:index + 1, :] * (-1.0 / 64), (8, LANES))
    coarse = lax.broadcasted_iota(jnp.int32, (LANES, LANES), 0) * lax.broadcasted_iota(jnp.int32, (LANES, LANES), 1)
    dft_cos, dft_sin = unit_circle(jnp.bitwise_and(coarse, LANES - 1), LANES)
    for part, tables in enumerate(((dft_cos, dft_sin), (-dft_sin, dft_cos))):
        for half, table in enumerate(tables):
            place = (slice(part * LANES, part * LANES + LANES), slice(half * LANES, half * LANES + LANES))
            high = table.astype(jnp.bfloat16)
            dft_high[place] = high
            dft_low[place] = (table - high.astype(jnp.float32)).astype(jnp.bfloat16)
    sorted_row = lax.broadcasted_iota(jnp.int32, (256, 256), 0)
    came_row = lax.broadcasted_iota(jnp.int32, (256, 256), 1)
    wanted = jnp.bitwise_and(sorted_row, 30) * 8 + lax.shift_right_logical(sorted_row, 5) * 2 + jnp.bitwise_and(sorted_row, 1)
    spread[...] = (wanted == came_row).astype(jnp.float32).astype(jnp.bfloat16)

    def order_copy(step):
        return pltpu.make_async_remote_copy(
            src_ref=own_order,
            dst_ref=orders.at[blk],
            send_sem=order_sem.at[0],
            recv_sem=order_sem.at[1],
            device_id=(freq, lax.rem(blk + step, 8)),
            device_id_type=MESH,
        )

    def half_rows(half):
        return pl.ds(pl.multiple_of(half * 16, 16), 16)

    first = lax.rem(side + core, 2)
    second = 1 - first

    def send_piece(group, part, half, other_freq, other_side, other_col):
        pltpu.make_async_remote_copy(
            src_ref=pieces.at[group, other_freq * 8 + other_col * 2 + other_side, part],
            dst_ref=arrived.at[group, me, part],
            send_sem=send_sem.at[half, group],
            recv_sem=recv_sem.at[half, group],
            device_id=(other_freq, other_side * 4 + other_col),
            device_id_type=MESH,
        ).start()

    def own_piece(group):
        return pltpu.make_async_copy(pieces.at[group, freq * 8 + channel], arrived.at[group, me], own_sem.at[group])

    def wait_pieces(group, part, half, sems):
        place = (group, pl.ds(0, 127), part)
        pltpu.make_async_copy(pieces.at[place], arrived.at[place], sems.at[half, group]).wait()

    def group_step(group, carry):
        @pl.when(group == 0)
        def _():
            load(0).wait()

        @pl.when(group > 0)
        def _():
            load(group).wait()

        def filter_column(index, carry):
            weights = [jnp.broadcast_to(taps[pl.ds(t, 1), pl.ds(pl.multiple_of(index * LANES, LANES), LANES)], (16, LANES)) for t in range(TAPS)]
            for part in range(2):
                frames = []
                for frame in range(GROUP + TAPS - 1):
                    start = pl.multiple_of((group * GROUP + frame) * CH + index * LANES, LANES)
                    frames.append(volt[part, :, pl.ds(start, LANES)].astype(jnp.float32))
                for spec in range(GROUP):
                    total = weights[0] * frames[spec]
                    for tap in range(1, TAPS):
                        total = total + weights[tap] * frames[spec + tap]
                    filt[part, spec, index] = total.astype(jnp.bfloat16).astype(jnp.float32)
            return carry

        lax.fori_loop(0, COLS, filter_column, 0)

        for spec in range(GROUP):
            for half in range(2):
                rows_half = slice(half * 8, half * 8 + 8)
                values = []
                for index in range(COLS):
                    values.append(tuple(filt[part, spec, index, rows_half] for part in range(2)))
                for index, (real, imag) in enumerate(fft_columns(values)):
                    cos, sin = turn_cos[index], turn_sin[index]
                    place = pl.ds(half * LANES + spec * COLS + index, 8, stride=Z_STRIDE)
                    z_real[place, :] = real * cos - imag * sin
                    z_imag[place, :] = real * sin + imag * cos

        def last_step(block, carry):
            block_rows = pl.ds(pl.multiple_of(block * Z_STRIDE, 8), 256)
            both = jnp.concatenate([z_real[block_rows, :], z_imag[block_rows, :]], axis=1)
            high = both.astype(jnp.bfloat16)
            low = (both - high.astype(jnp.float32)).astype(jnp.bfloat16)
            total = lax.dot_general(dft_high[...], high, CONTRACT_LAST, preferred_element_type=jnp.float32)
            total = total + lax.dot_general(dft_low[...], high, CONTRACT_LAST, preferred_element_type=jnp.float32)
            total = total + lax.dot_general(dft_high[...], low, CONTRACT_LAST, preferred_element_type=jnp.float32)
            for part in range(2):
                for half in range(2):
                    piece = total[part * 128:part * 128 + 128, half * 128:half * 128 + 128]
                    wide[pl.ds(block * 4 + part * 2 + half, 128, stride=WIDE_STRIDE), :] = piece
            return carry

        lax.fori_loop(0, 8, last_step, 0, unroll=2)

        def narrow(index, carry):
            for sub in range(8):
                wide_rows = pl.ds(pl.multiple_of((index * 8 + sub) * WIDE_STRIDE, 8), 32)
                pieces[group, index * 8 + sub] = wide[wide_rows, :].astype(jnp.bfloat16)
            return carry

        lax.fori_loop(0, 16, narrow, 0)

        @pl.when(group == 0)
        def _():
            pl.semaphore_wait(barrier, 127)
            for step in range(1, 8):
                order_copy(step).start()

        @pl.when(group < WHOLE_GROUPS)
        def _():
            def send(other_freq, other_side, other_col):
                send_piece(group, slice(None), 0, other_freq, other_side, other_col)

            visit_others(send)

        @pl.when(group >= WHOLE_GROUPS)
        def _():
            def send(other_freq, other_side, other_col):
                send_piece(group, half_rows(lax.rem(other_side + lax.rem(other_freq, 2), 2)), 0, other_freq, other_side, other_col)

            visit_others(send)

        own_piece(group).start()
        return carry

    lax.fori_loop(0, GROUPS, group_step, 0)

    def send_rest(group, carry):
        def send(other_freq, other_side, other_col):
            send_piece(group, half_rows(lax.rem(1 + other_side + lax.rem(other_freq, 2), 2)), 1, other_freq, other_side, other_col)

        visit_others(send)
        return carry

    lax.fori_loop(WHOLE_GROUPS, GROUPS, send_rest, 0)

    orders[blk] = own_order[...]
    for sem in range(2):
        pltpu.make_async_copy(orders.at[pl.ds(0, 7)], orders.at[pl.ds(0, 7)], order_sem.at[sem]).wait()
    members = lax.broadcasted_iota(jnp.int32, (256, 256), 0)
    for member in range(8):
        flags = (orders[member, 0:1, :] == members).astype(jnp.float32)
        chosen[member] = flags.T.astype(jnp.bfloat16)

    def take_half(group, half):
        def unshuffle(index, carry):
            lanes = jnp.concatenate(
                [
                    arrived[group, pl.ds(pl.multiple_of(index * 32 + step * 16, 16), 16), half_rows(half)].reshape(256, LANES)
                    for step in range(2)
                ],
                axis=1,
            )
            sorted_rows = jnp.dot(spread[...], lanes, preferred_element_type=jnp.float32).astype(jnp.bfloat16)
            for member in range(4):
                for part in range(2):
                    start = member * 64 + part * 32
                    for step in range(2):
                        place = pl.ds(pl.multiple_of(index * 64 + step * 32, 32), 32)
                        natural[half * 4 + member, place, part * LANES:part * LANES + LANES] = sorted_rows[start:start + 32, step * LANES:step * LANES + LANES]
            return carry

        lax.fori_loop(0, 4, unshuffle, 0, unroll=4)

        def arrange(index, carry):
            member = half * 4 + index
            picked = jnp.dot(chosen[member], natural[member], preferred_element_type=jnp.float32).astype(jnp.bfloat16)
            for part in range(2):
                rows[member, part * GROUPS + group] = picked[:, part * LANES:part * LANES + LANES]
            return carry

        lax.fori_loop(0, 4, arrange, 0, unroll=4)

    def take_whole(group, carry):
        own_piece(group).wait()
        wait_pieces(group, slice(None), 0, recv_sem)
        for half in range(2):
            take_half(group, half)
        return carry

    lax.fori_loop(0, WHOLE_GROUPS, take_whole, 0)

    def take_first(group, carry):
        own_piece(group).wait()
        wait_pieces(group, pl.ds(0, 16), 0, recv_sem)
        take_half(group, first)
        return carry

    lax.fori_loop(WHOLE_GROUPS, GROUPS, take_first, 0)

    def side_of(member, part):
        return jnp.concatenate([rows[member, part * GROUPS + group] for group in range(GROUPS)], axis=1)

    def product(left, right):
        return lax.dot_general(left, right, CONTRACT_LAST, preferred_element_type=jnp.float32)

    def correlate(member, other):
        left_real, left_imag = side_of(member, 0), side_of(member, 1)
        right_real, right_imag = side_of(other, 0), side_of(other, 1)
        real = product(left_real, right_real) + product(left_imag, right_imag)
        imag = product(left_imag, right_real) - product(left_real, right_imag)
        return real * (1.0 / 512), imag * (1.0 / 512)

    def post(is_own, dest, source, place, send, receive, own):
        @pl.when(is_own)
        def _():
            pltpu.make_async_copy(source, place, own).start()

        @pl.when(jnp.logical_not(is_own))
        def _():
            pltpu.make_async_remote_copy(
                src_ref=source, dst_ref=place, send_sem=send, recv_sem=receive, device_id=(freq, dest), device_id_type=MESH
            ).start()

    def turn_target(turn):
        step = lax.rem(turn * 5 + 1, 8)
        return step, lax.rem(side + step // 4, 2) * 4 + lax.rem(col + lax.rem(step, 4), 4)

    def send_near(is_own, dest, lag):
        values = correlate(dest, lax.rem(dest + lag, 8))
        for part in range(2):
            place = (lag - 1) * 2 + part
            tiles[dest, place] = values[part].astype(jnp.bfloat16)
            post(is_own, dest, tiles.at[dest, place], near.at[channel, place], tile_sem.at[0], tile_sem.at[1], tile_sem.at[2])

    def send_packed(is_own, dest):
        real, imag = correlate(dest, dest)
        down = lax.broadcasted_iota(jnp.int32, (256, 256), 0)
        across = lax.broadcasted_iota(jnp.int32, (256, 256), 1)
        tiles[dest, 6] = jnp.where(down >= across, real, imag).astype(jnp.bfloat16)
        post(is_own, dest, tiles.at[dest, 6], packed.at[channel], tile_sem.at[6], tile_sem.at[7], tile_sem.at[8])

    def early_packed(index, carry):
        dest = first * 4 + lax.rem(col + index + 1, 4)
        send_packed(dest == blk, dest)
        return carry

    lax.fori_loop(0, 4, early_packed, 0)

    def early_near(index, carry):
        lag = lax.div(index, 4) + 1
        dest_col = lax.rem(col + lax.rem(index, 4) + 1, 4)
        dest = first * 4 + dest_col

        @pl.when(dest_col + lag < 4)
        def _():
            send_near(dest == blk, dest, lag)

        return carry

    lax.fori_loop(0, 4, early_near, 0)

    def take_second(group, carry):
        wait_pieces(group, pl.ds(16, 16), 1, recv_sem)
        take_half(group, second)
        return carry

    lax.fori_loop(WHOLE_GROUPS, GROUPS, take_second, 0)

    def near_step(index, carry):
        lag = lax.div(index, 8) + 1
        step, dest = turn_target(lax.rem(index, 8))

        @pl.when(jnp.logical_or(lax.div(dest, 4) != first, jnp.logical_or(lag > 1, lax.rem(dest, 4) + lag >= 4)))
        def _():
            send_near(step == 0, dest, lag)

        return carry

    def late_packed(index, carry):
        dest = second * 4 + lax.rem(col + index + 1, 4)
        send_packed(dest == blk, dest)
        return carry

    lax.fori_loop(0, 16, near_step, 0)
    lax.fori_loop(0, 4, late_packed, 0)
    lax.fori_loop(16, 24, near_step, 0)

    def far_step(index, carry):
        step = lax.rem(index + 1, 4)
        dest = side * 4 + lax.rem(col + step, 4)
        values = correlate(dest, lax.rem(dest + 4, 8))
        for part in range(2):
            far_tiles[index, part] = values[part].astype(jnp.bfloat16)
            post(step == 0, dest, far_tiles.at[index, part], far.at[col, part], tile_sem.at[3], tile_sem.at[4], tile_sem.at[5])
        return carry

    lax.fori_loop(0, 4, far_step, 0)

    def finish_whole(group, carry):
        wait_pieces(group, slice(None), 0, send_sem)
        return carry

    def finish_halves(group, carry):
        for half in range(2):
            wait_pieces(group, pl.ds(half * 16, 16), half, send_sem)
        return carry

    lax.fori_loop(0, WHOLE_GROUPS, finish_whole, 0)
    lax.fori_loop(WHOLE_GROUPS, GROUPS, finish_halves, 0)

    pltpu.make_async_copy(tiles.at[0, 6], packed.at[0], tile_sem.at[8]).wait()
    for sem in (6, 7):
        pltpu.make_async_copy(packed.at[pl.ds(0, 7)], packed.at[pl.ds(0, 7)], tile_sem.at[sem]).wait()

    def unpack(index, carry):
        triangles = packed[index].astype(jnp.float32)
        turned = triangles.T
        down = lax.broadcasted_iota(jnp.int32, (256, 256), 0)
        across = lax.broadcasted_iota(jnp.int32, (256, 256), 1)
        unpacked[index, 0] = jnp.where(down >= across, triangles, turned).astype(jnp.bfloat16)
        mirrored = jnp.where(down > across, -turned, 0.0)
        unpacked[index, 1] = jnp.where(down < across, triangles, mirrored).astype(jnp.bfloat16)
        return carry

    lax.fori_loop(0, 8, unpack, 0)
    unpacked_copy = pltpu.make_async_copy(unpacked, mirror, tile_sem.at[9])
    unpacked_copy.start()
    unpacked_copy.wait()

    whole_parts = pl.ds(0, 6)
    pltpu.make_async_copy(tiles.at[0, whole_parts], near.at[0, whole_parts], tile_sem.at[2]).wait()
    for sem in (0, 1):
        pltpu.make_async_copy(tiles.at[pl.ds(0, 7), whole_parts], near.at[pl.ds(0, 7), whole_parts], tile_sem.at[sem]).wait()
    pltpu.make_async_copy(far_tiles.at[0], far.at[0], tile_sem.at[5]).wait()
    for sem in (3, 4):
        pltpu.make_async_copy(far_tiles.at[pl.ds(0, 3)], far.at[pl.ds(0, 3)], tile_sem.at[sem]).wait()


def make_tiles(voltages, pfb_taps, order_table):
    anywhere = pl.BlockSpec(memory_space=pl.ANY)
    return pl.pallas_call(
        correlator_kernel,
        out_shape=(
            jax.ShapeDtypeStruct((8, 6, 256, 256), jnp.bfloat16),
            jax.ShapeDtypeStruct((8, 2, 256, 256), jnp.bfloat16),
            jax.ShapeDtypeStruct((4, 2, 256, 256), jnp.bfloat16),
        ),
        in_specs=[anywhere] + [pl.BlockSpec(memory_space=pltpu.VMEM)] * 2,
        out_specs=(anywhere, anywhere, anywhere),
        scratch_shapes=[pltpu.VMEM(voltages.shape, jnp.bfloat16)]
        + [
            pltpu.VMEM((COLS, 8, LANES), jnp.float32),
            pltpu.VMEM((COLS, 8, LANES), jnp.float32),
            pltpu.VMEM((256, 256), jnp.bfloat16),
            pltpu.VMEM((256, 256), jnp.bfloat16),
            pltpu.VMEM((256, 256), jnp.bfloat16),
            pltpu.VMEM((2, GROUP, COLS, 16, LANES), jnp.float32),
            pltpu.VMEM((8 * Z_STRIDE, LANES), jnp.float32),
            pltpu.VMEM((8 * Z_STRIDE, LANES), jnp.float32),
            pltpu.VMEM((128 * WIDE_STRIDE, LANES), jnp.float32),
            pltpu.VMEM((GROUPS, 128, 32, LANES), jnp.bfloat16),
            pltpu.VMEM((GROUPS, 128, 32, LANES), jnp.bfloat16),
            pltpu.VMEM((8, 256), jnp.int32),
            pltpu.VMEM((8, 8, 256), jnp.int32),
            pltpu.VMEM((8, 256, 256), jnp.bfloat16),
            pltpu.VMEM((8, 256, 256), jnp.bfloat16),
            pltpu.VMEM((8, 8, 256, LANES), jnp.bfloat16),
            pltpu.VMEM((8, 7, 256, 256), jnp.bfloat16),
            pltpu.VMEM((4, 2, 256, 256), jnp.bfloat16),
            pltpu.VMEM((8, 256, 256), jnp.bfloat16),
            pltpu.VMEM((8, 2, 256, 256), jnp.bfloat16),
            pltpu.SemaphoreType.DMA((GROUPS,)),
            pltpu.SemaphoreType.DMA((2, GROUPS)),
            pltpu.SemaphoreType.DMA((2, GROUPS)),
            pltpu.SemaphoreType.DMA((GROUPS,)),
            pltpu.SemaphoreType.DMA((2,)),
            pltpu.SemaphoreType.DMA((10,)),
        ],
        compiler_params=pltpu.CompilerParams(vmem_limit_bytes=44 * 2**20, collective_id=0, has_side_effects=True),
        cost_estimate=pl.CostEstimate(flops=10**10, bytes_accessed=16 * 2**20, transcendentals=0),
    )(voltages, order_table, pfb_taps)


def arrange_kernel(lag_table, near, mirror, far, visibility, far_visibility, sems):
    far_copy = pltpu.make_async_copy(far, far_visibility.at[:, 0], sems.at[0])
    far_copy.start()
    for slot in range(4):
        lag = lag_table[slot]

        @pl.when(lag == 0)
        def _(slot=slot):
            for out in range(8):
                pltpu.make_async_copy(mirror.at[out], visibility.at[out, 0, slot], sems.at[slot + 1]).start()

        @pl.when(lag > 0)
        def _(slot=slot, lag=lag):
            for out in range(8):
                pltpu.make_async_copy(near.at[out, pl.ds((lag - 1) * 2, 2)], visibility.at[out, 0, slot], sems.at[slot + 1]).start()

    for slot in range(4):
        pltpu.make_async_copy(mirror, visibility.at[:, 0, slot], sems.at[slot + 1]).wait()
    far_copy.wait()


def arrange(near, mirror, far, lag_table):
    return pl.pallas_call(
        arrange_kernel,
        out_shape=(
            jax.ShapeDtypeStruct((8, 1, 4, 2, 256, 256), jnp.bfloat16),
            jax.ShapeDtypeStruct((4, 1, 2, 256, 256), jnp.bfloat16),
        ),
        in_specs=[pl.BlockSpec(memory_space=pltpu.SMEM)] + [pl.BlockSpec(memory_space=pltpu.VMEM)] * 3,
        out_specs=(pl.BlockSpec(memory_space=pl.ANY), pl.BlockSpec(memory_space=pl.ANY)),
        scratch_shapes=[pltpu.SemaphoreType.DMA((5,))],
        compiler_params=pltpu.CompilerParams(vmem_limit_bytes=2**20),
    )(lag_table, near, mirror, far)


def per_device(voltages, pfb_taps, order_table, lag_table):
    near, mirror, far = make_tiles(voltages, pfb_taps, order_table)
    return arrange(near, mirror, far, lag_table)


def solution(mesh):
    placed = (P(None, ("freq", "blk"), None), P(), P("blk", None), P())
    return jax.shard_map(
        per_device,
        mesh=mesh,
        in_specs=placed,
        out_specs=(P("freq", "blk", None, None, None, None), P("freq", "blk", None, None, None)),
        check_vma=False,
    )
```

```python
import functools
import math

import jax
import jax.numpy as jnp
import numpy as np
from jax import lax
from jax.experimental import pallas as pl
from jax.experimental.pallas import tpu as pltpu
from jax.sharding import PartitionSpec as P

CH = 4096
TAPS = 16
SPECTRA = 16
COLS = 32
LANES = 128
GROUP = 4
GROUPS = 4
WHOLE_GROUPS = 1
Z_STRIDE = 264
WIDE_STRIDE = 40


def complex_mul(value, turn):
    real, imag = value
    cos, sin = float(turn.real), float(turn.imag)
    if abs(sin) < 1e-12 and abs(cos - 1) < 1e-12:
        return value
    if abs(cos) < 1e-12 and abs(sin + 1) < 1e-12:
        return (imag, -real)
    if abs(cos + sin) < 1e-12:
        return ((real + imag) * cos, (imag - real) * cos)
    if abs(cos - sin) < 1e-12:
        return ((real - imag) * cos, (real + imag) * cos)
    return (real * cos - imag * sin, real * sin + imag * cos)


def fft_list(values):
    count = len(values)
    if count == 1:
        return values
    if count == 2:
        (ar, ai), (br, bi) = values
        return [(ar + br, ai + bi), (ar - br, ai - bi)]
    if count == 4:
        even = fft_list([values[0], values[2]])
        odd = fft_list([values[1], values[3]])
    else:
        even = fft_list(values[0::2])
        odd = fft_list(values[1::2])
    half = count // 2
    low, high = [], []
    for index in range(half):
        turned = complex_mul(odd[index], np.exp(-2j * np.pi * index / count))
        base = even[index]
        low.append((base[0] + turned[0], base[1] + turned[1]))
        high.append((base[0] - turned[0], base[1] - turned[1]))
    return low + high


def fft_columns(values):
    sections = []
    for low in range(8):
        parts = fft_list([values[8 * high + low] for high in range(4)])
        sections.append([complex_mul(part, np.exp(-2j * np.pi * low * index / 32)) for index, part in enumerate(parts)])
    result = [None] * 32
    for index in range(4):
        parts = fft_list([sections[low][index] for low in range(8)])
        for high in range(8):
            result[index + 4 * high] = parts[high]
    return result


MESH = pl.DeviceIdType.MESH
CONTRACT_LAST = (((1,), (1,)), ((), ()))


def position():
    freq = lax.axis_index("freq")
    blk = lax.axis_index("blk")
    return (lax.rem(blk, 4), lax.rem(freq // 2, 2) * 2 + blk // 4, freq // 4, lax.rem(freq, 2))


def mesh_ids(col, row, layer, core):
    return (layer * 4 + (row // 2) * 2 + core, lax.rem(row, 2) * 4 + col)


def unit_circle(steps, count):
    centered = jnp.where(steps > count // 2, steps - count, steps).astype(jnp.float32)
    angle = centered * (2 * math.pi / count)
    square = angle * angle
    cos = jnp.zeros_like(angle)
    sin = jnp.zeros_like(angle)
    for order in range(9, -1, -1):
        cos = cos * square + (-1) ** order / math.factorial(2 * order)
        sin = sin * square + (-1) ** order / math.factorial(2 * order + 1)
    return cos, sin * angle


def correlator_kernel(
    volt_far, order_row, taps,
    near, mirror, far,
    volt, turn_cos, turn_sin, dft_high, dft_low, spread,
    filt, z_real, z_imag, wide, pieces, arrived, own_order, orders, chosen, natural, rows, tiles, far_tiles, packed, unpacked,
    load_sem, send_sem, recv_sem, own_sem, order_sem, tile_sem,
):
    def load(group):
        first = 0 if isinstance(group, int) else pl.multiple_of((group * GROUP + TAPS - 1) * CH, LANES)
        size = (GROUP + TAPS - 1) * CH if isinstance(group, int) else GROUP * CH
        place = (slice(None), slice(None), pl.ds(first, size))
        return pltpu.make_async_copy(volt_far.at[place], volt.at[place], load_sem.at[group])

    load(0).start()
    for later in range(1, GROUPS):
        load(jnp.int32(later)).start()

    col, row, layer, core = position()
    freq, blk = mesh_ids(col, row, layer, core)
    me = freq * 8 + blk
    side = blk // 4
    channel = col * 2 + side

    def visit_others(visit):
        cols = [lax.rem(col + step, 4) for step in range(4)]

        def visit_plane(index, carry):
            new_row = lax.rem(row + lax.rem(index, 4), 4)
            new_layer = lax.rem(layer + lax.rem(lax.div(index, 4), 4), 4)
            new_core = lax.rem(core + lax.div(index, 16), 2)
            other_freq = new_layer * 4 + lax.div(new_row, 2) * 2 + new_core
            other_side = lax.rem(new_row, 2)

            @pl.when(index > 0)
            def _():
                visit(other_freq, other_side, cols[0])

            for step in range(1, 4):
                visit(other_freq, other_side, cols[step])
            return carry

        lax.fori_loop(0, 32, visit_plane, 0)

    barrier = pltpu.get_barrier_semaphore()

    def greet(other_freq, other_side, other_col):
        pl.semaphore_signal(barrier, inc=1, device_id=(other_freq, other_side * 4 + other_col), device_id_type=MESH)

    visit_others(greet)
    own_order[...] = jnp.broadcast_to(order_row[...], (8, 256))
    fine = lax.broadcasted_iota(jnp.int32, (COLS, LANES), 0) * lax.broadcasted_iota(jnp.int32, (COLS, LANES), 1)
    fine_cos, fine_sin = unit_circle(fine, CH)
    for index in range(COLS):
        turn_cos[index] = jnp.broadcast_to(fine_cos[index:index + 1, :] * (1.0 / 64), (8, LANES))
        turn_sin[index] = jnp.broadcast_to(fine_sin[index:index + 1, :] * (-1.0 / 64), (8, LANES))
    coarse = lax.broadcasted_iota(jnp.int32, (LANES, LANES), 0) * lax.broadcasted_iota(jnp.int32, (LANES, LANES), 1)
    dft_cos, dft_sin = unit_circle(jnp.bitwise_and(coarse, LANES - 1), LANES)
    for part, tables in enumerate(((dft_cos, dft_sin), (-dft_sin, dft_cos))):
        for half, table in enumerate(tables):
            place = (slice(part * LANES, part * LANES + LANES), slice(half * LANES, half * LANES + LANES))
            high = table.astype(jnp.bfloat16)
            dft_high[place] = high
            dft_low[place] = (table - high.astype(jnp.float32)).astype(jnp.bfloat16)
    sorted_row = lax.broadcasted_iota(jnp.int32, (256, 256), 0)
    came_row = lax.broadcasted_iota(jnp.int32, (256, 256), 1)
    wanted = jnp.bitwise_and(sorted_row, 30) * 8 + lax.shift_right_logical(sorted_row, 5) * 2 + jnp.bitwise_and(sorted_row, 1)
    spread[...] = (wanted == came_row).astype(jnp.float32).astype(jnp.bfloat16)

    def order_copy(step):
        return pltpu.make_async_remote_copy(
            src_ref=own_order,
            dst_ref=orders.at[blk],
            send_sem=order_sem.at[0],
            recv_sem=order_sem.at[1],
            device_id=(freq, lax.rem(blk + step, 8)),
            device_id_type=MESH,
        )

    def half_rows(half):
        return pl.ds(pl.multiple_of(half * 16, 16), 16)

    first = lax.rem(side + core, 2)
    second = 1 - first

    def send_piece(group, part, half, other_freq, other_side, other_col):
        pltpu.make_async_remote_copy(
            src_ref=pieces.at[group, other_freq * 8 + other_col * 2 + other_side, part],
            dst_ref=arrived.at[group, me, part],
            send_sem=send_sem.at[half, group],
            recv_sem=recv_sem.at[half, group],
            device_id=(other_freq, other_side * 4 + other_col),
            device_id_type=MESH,
        ).start()

    def own_piece(group):
        return pltpu.make_async_copy(pieces.at[group, freq * 8 + channel], arrived.at[group, me], own_sem.at[group])

    def wait_pieces(group, part, half, sems):
        place = (group, pl.ds(0, 127), part)
        pltpu.make_async_copy(pieces.at[place], arrived.at[place], sems.at[half, group]).wait()

    def group_step(group, carry):
        @pl.when(group == 0)
        def _():
            load(0).wait()

        @pl.when(group > 0)
        def _():
            load(group).wait()

        def filter_column(index, carry):
            weights = [jnp.broadcast_to(taps[pl.ds(t, 1), pl.ds(pl.multiple_of(index * LANES, LANES), LANES)], (16, LANES)) for t in range(TAPS)]
            for part in range(2):
                frames = []
                for frame in range(GROUP + TAPS - 1):
                    start = pl.multiple_of((group * GROUP + frame) * CH + index * LANES, LANES)
                    frames.append(volt[part, :, pl.ds(start, LANES)].astype(jnp.float32))
                for spec in range(GROUP):
                    total = weights[0] * frames[spec]
                    for tap in range(1, TAPS):
                        total = total + weights[tap] * frames[spec + tap]
                    filt[part, spec, index] = total.astype(jnp.bfloat16).astype(jnp.float32)
            return carry

        lax.fori_loop(0, COLS, filter_column, 0)

        for spec in range(GROUP):
            for half in range(2):
                rows_half = slice(half * 8, half * 8 + 8)
                values = []
                for index in range(COLS):
                    values.append(tuple(filt[part, spec, index, rows_half] for part in range(2)))
                for index, (real, imag) in enumerate(fft_columns(values)):
                    cos, sin = turn_cos[index], turn_sin[index]
                    place = pl.ds(half * LANES + spec * COLS + index, 8, stride=Z_STRIDE)
                    z_real[place, :] = real * cos - imag * sin
                    z_imag[place, :] = real * sin + imag * cos

        def last_step(block, carry):
            block_rows = pl.ds(pl.multiple_of(block * Z_STRIDE, 8), 256)
            both = jnp.concatenate([z_real[block_rows, :], z_imag[block_rows, :]], axis=1)
            high = both.astype(jnp.bfloat16)
            low = (both - high.astype(jnp.float32)).astype(jnp.bfloat16)
            total = lax.dot_general(dft_high[...], high, CONTRACT_LAST, preferred_element_type=jnp.float32)
            total = total + lax.dot_general(dft_low[...], high, CONTRACT_LAST, preferred_element_type=jnp.float32)
            total = total + lax.dot_general(dft_high[...], low, CONTRACT_LAST, preferred_element_type=jnp.float32)
            for part in range(2):
                for half in range(2):
                    piece = total[part * 128:part * 128 + 128, half * 128:half * 128 + 128]
                    wide[pl.ds(block * 4 + part * 2 + half, 128, stride=WIDE_STRIDE), :] = piece
            return carry

        lax.fori_loop(0, 8, last_step, 0, unroll=2)

        def narrow(index, carry):
            for sub in range(8):
                wide_rows = pl.ds(pl.multiple_of((index * 8 + sub) * WIDE_STRIDE, 8), 32)
                pieces[group, index * 8 + sub] = wide[wide_rows, :].astype(jnp.bfloat16)
            return carry

        lax.fori_loop(0, 16, narrow, 0)

        @pl.when(group == 0)
        def _():
            pl.semaphore_wait(barrier, 127)
            for step in range(1, 8):
                order_copy(step).start()

        @pl.when(group < WHOLE_GROUPS)
        def _():
            def send(other_freq, other_side, other_col):
                send_piece(group, slice(None), 0, other_freq, other_side, other_col)

            visit_others(send)

        @pl.when(group >= WHOLE_GROUPS)
        def _():
            def send(other_freq, other_side, other_col):
                send_piece(group, half_rows(lax.rem(other_side + lax.rem(other_freq, 2), 2)), 0, other_freq, other_side, other_col)

            visit_others(send)

        own_piece(group).start()
        return carry

    lax.fori_loop(0, GROUPS, group_step, 0)

    def send_rest(group, carry):
        def send(other_freq, other_side, other_col):
            send_piece(group, half_rows(lax.rem(1 + other_side + lax.rem(other_freq, 2), 2)), 1, other_freq, other_side, other_col)

        visit_others(send)
        return carry

    lax.fori_loop(WHOLE_GROUPS, GROUPS, send_rest, 0)

    orders[blk] = own_order[...]
    for sem in range(2):
        pltpu.make_async_copy(orders.at[pl.ds(0, 7)], orders.at[pl.ds(0, 7)], order_sem.at[sem]).wait()
    members = lax.broadcasted_iota(jnp.int32, (256, 256), 0)
    for member in range(8):
        flags = (orders[member, 0:1, :] == members).astype(jnp.float32)
        chosen[member] = flags.T.astype(jnp.bfloat16)

    def take_half(group, half):
        def unshuffle(index, carry):
            lanes = jnp.concatenate(
                [
                    arrived[group, pl.ds(pl.multiple_of(index * 32 + step * 16, 16), 16), half_rows(half)].reshape(256, LANES)
                    for step in range(2)
                ],
                axis=1,
            )
            sorted_rows = jnp.dot(spread[...], lanes, preferred_element_type=jnp.float32).astype(jnp.bfloat16)
            for member in range(4):
                for part in range(2):
                    start = member * 64 + part * 32
                    for step in range(2):
                        place = pl.ds(pl.multiple_of(index * 64 + step * 32, 32), 32)
                        natural[half * 4 + member, place, part * LANES:part * LANES + LANES] = sorted_rows[start:start + 32, step * LANES:step * LANES + LANES]
            return carry

        lax.fori_loop(0, 4, unshuffle, 0, unroll=4)

        def arrange(index, carry):
            member = half * 4 + index
            picked = jnp.dot(chosen[member], natural[member], preferred_element_type=jnp.float32).astype(jnp.bfloat16)
            for part in range(2):
                rows[member, part * GROUPS + group] = picked[:, part * LANES:part * LANES + LANES]
            return carry

        lax.fori_loop(0, 4, arrange, 0, unroll=4)

    def take_whole(group, carry):
        own_piece(group).wait()
        wait_pieces(group, slice(None), 0, recv_sem)
        for half in range(2):
            take_half(group, half)
        return carry

    lax.fori_loop(0, WHOLE_GROUPS, take_whole, 0)

    def take_first(group, carry):
        own_piece(group).wait()
        wait_pieces(group, pl.ds(0, 16), 0, recv_sem)
        take_half(group, first)
        return carry

    lax.fori_loop(WHOLE_GROUPS, GROUPS, take_first, 0)

    def side_of(member, part):
        return jnp.concatenate([rows[member, part * GROUPS + group] for group in range(GROUPS)], axis=1)

    def product(left, right):
        return lax.dot_general(left, right, CONTRACT_LAST, preferred_element_type=jnp.float32)

    def correlate(member, other):
        left_real, left_imag = side_of(member, 0), side_of(member, 1)
        right_real, right_imag = side_of(other, 0), side_of(other, 1)
        real = product(left_real, right_real) + product(left_imag, right_imag)
        imag = product(left_imag, right_real) - product(left_real, right_imag)
        return real * (1.0 / 512), imag * (1.0 / 512)

    def post(is_own, dest, source, place, send, receive, own):
        @pl.when(is_own)
        def _():
            pltpu.make_async_copy(source, place, own).start()

        @pl.when(jnp.logical_not(is_own))
        def _():
            pltpu.make_async_remote_copy(
                src_ref=source, dst_ref=place, send_sem=send, recv_sem=receive, device_id=(freq, dest), device_id_type=MESH
            ).start()

    def turn_target(turn):
        step = lax.rem(turn * 5 + 1, 8)
        return step, lax.rem(side + step // 4, 2) * 4 + lax.rem(col + lax.rem(step, 4), 4)

    def send_near(is_own, dest, lag):
        values = correlate(dest, lax.rem(dest + lag, 8))
        for part in range(2):
            place = (lag - 1) * 2 + part
            tiles[dest, place] = values[part].astype(jnp.bfloat16)
            post(is_own, dest, tiles.at[dest, place], near.at[channel, place], tile_sem.at[0], tile_sem.at[1], tile_sem.at[2])

    def send_packed(is_own, dest):
        real, imag = correlate(dest, dest)
        down = lax.broadcasted_iota(jnp.int32, (256, 256), 0)
        across = lax.broadcasted_iota(jnp.int32, (256, 256), 1)
        tiles[dest, 6] = jnp.where(down >= across, real, imag).astype(jnp.bfloat16)
        post(is_own, dest, tiles.at[dest, 6], packed.at[channel], tile_sem.at[6], tile_sem.at[7], tile_sem.at[8])

    def early_packed(index, carry):
        dest = first * 4 + lax.rem(col + index + 1, 4)
        send_packed(dest == blk, dest)
        return carry

    lax.fori_loop(0, 4, early_packed, 0)

    def early_near(index, carry):
        lag = lax.div(index, 4) + 1
        dest_col = lax.rem(col + lax.rem(index, 4) + 1, 4)
        dest = first * 4 + dest_col

        @pl.when(dest_col + lag < 4)
        def _():
            send_near(dest == blk, dest, lag)

        return carry

    lax.fori_loop(0, 4, early_near, 0)

    def take_second(group, carry):
        wait_pieces(group, pl.ds(16, 16), 1, recv_sem)
        take_half(group, second)
        return carry

    lax.fori_loop(WHOLE_GROUPS, GROUPS, take_second, 0)

    def near_step(index, carry):
        lag = lax.div(index, 8) + 1
        step, dest = turn_target(lax.rem(index, 8))

        @pl.when(jnp.logical_or(lax.div(dest, 4) != first, jnp.logical_or(lag > 1, lax.rem(dest, 4) + lag >= 4)))
        def _():
            send_near(step == 0, dest, lag)

        return carry

    def late_packed(index, carry):
        dest = second * 4 + lax.rem(col + index + 1, 4)
        send_packed(dest == blk, dest)
        return carry

    lax.fori_loop(0, 16, near_step, 0)
    lax.fori_loop(0, 4, late_packed, 0)
    lax.fori_loop(16, 24, near_step, 0)

    def far_step(index, carry):
        step = lax.rem(index + 1, 4)
        dest = side * 4 + lax.rem(col + step, 4)
        values = correlate(dest, lax.rem(dest + 4, 8))
        for part in range(2):
            far_tiles[index, part] = values[part].astype(jnp.bfloat16)
            post(step == 0, dest, far_tiles.at[index, part], far.at[col, part], tile_sem.at[3], tile_sem.at[4], tile_sem.at[5])
        return carry

    lax.fori_loop(0, 4, far_step, 0)

    def finish_whole(group, carry):
        wait_pieces(group, slice(None), 0, send_sem)
        return carry

    def finish_halves(group, carry):
        for half in range(2):
            wait_pieces(group, pl.ds(half * 16, 16), half, send_sem)
        return carry

    lax.fori_loop(0, WHOLE_GROUPS, finish_whole, 0)
    lax.fori_loop(WHOLE_GROUPS, GROUPS, finish_halves, 0)

    pltpu.make_async_copy(tiles.at[0, 6], packed.at[0], tile_sem.at[8]).wait()
    for sem in (6, 7):
        pltpu.make_async_copy(packed.at[pl.ds(0, 7)], packed.at[pl.ds(0, 7)], tile_sem.at[sem]).wait()

    def unpack(index, carry):
        triangles = packed[index].astype(jnp.float32)
        turned = triangles.T
        down = lax.broadcasted_iota(jnp.int32, (256, 256), 0)
        across = lax.broadcasted_iota(jnp.int32, (256, 256), 1)
        unpacked[index, 0] = jnp.where(down >= across, triangles, turned).astype(jnp.bfloat16)
        mirrored = jnp.where(down > across, -turned, 0.0)
        unpacked[index, 1] = jnp.where(down < across, triangles, mirrored).astype(jnp.bfloat16)
        return carry

    lax.fori_loop(0, 8, unpack, 0)
    unpacked_copy = pltpu.make_async_copy(unpacked, mirror, tile_sem.at[9])
    unpacked_copy.start()
    unpacked_copy.wait()

    whole_parts = pl.ds(0, 6)
    pltpu.make_async_copy(tiles.at[0, whole_parts], near.at[0, whole_parts], tile_sem.at[2]).wait()
    for sem in (0, 1):
        pltpu.make_async_copy(tiles.at[pl.ds(0, 7), whole_parts], near.at[pl.ds(0, 7), whole_parts], tile_sem.at[sem]).wait()
    pltpu.make_async_copy(far_tiles.at[0], far.at[0], tile_sem.at[5]).wait()
    for sem in (3, 4):
        pltpu.make_async_copy(far_tiles.at[pl.ds(0, 3)], far.at[pl.ds(0, 3)], tile_sem.at[sem]).wait()


def make_tiles(voltages, pfb_taps, order_table):
    anywhere = pl.BlockSpec(memory_space=pl.ANY)
    return pl.pallas_call(
        correlator_kernel,
        out_shape=(
            jax.ShapeDtypeStruct((8, 6, 256, 256), jnp.bfloat16),
            jax.ShapeDtypeStruct((8, 2, 256, 256), jnp.bfloat16),
            jax.ShapeDtypeStruct((4, 2, 256, 256), jnp.bfloat16),
        ),
        in_specs=[anywhere] + [pl.BlockSpec(memory_space=pltpu.VMEM)] * 2,
        out_specs=(anywhere, anywhere, anywhere),
        scratch_shapes=[pltpu.VMEM(voltages.shape, jnp.bfloat16)]
        + [
            pltpu.VMEM((COLS, 8, LANES), jnp.float32),
            pltpu.VMEM((COLS, 8, LANES), jnp.float32),
            pltpu.VMEM((256, 256), jnp.bfloat16),
            pltpu.VMEM((256, 256), jnp.bfloat16),
            pltpu.VMEM((256, 256), jnp.bfloat16),
            pltpu.VMEM((2, GROUP, COLS, 16, LANES), jnp.float32),
            pltpu.VMEM((9 * Z_STRIDE, LANES), jnp.float32),
            pltpu.VMEM((9 * Z_STRIDE, LANES), jnp.float32),
            pltpu.VMEM((129 * WIDE_STRIDE, LANES), jnp.float32),
            pltpu.VMEM((GROUPS, 128, 32, LANES), jnp.bfloat16),
            pltpu.VMEM((GROUPS, 128, 32, LANES), jnp.bfloat16),
            pltpu.VMEM((8, 256), jnp.int32),
            pltpu.VMEM((8, 8, 256), jnp.int32),
            pltpu.VMEM((8, 256, 256), jnp.bfloat16),
            pltpu.VMEM((8, 256, 256), jnp.bfloat16),
            pltpu.VMEM((8, 8, 256, LANES), jnp.bfloat16),
            pltpu.VMEM((8, 7, 256, 256), jnp.bfloat16),
            pltpu.VMEM((4, 2, 256, 256), jnp.bfloat16),
            pltpu.VMEM((8, 256, 256), jnp.bfloat16),
            pltpu.VMEM((8, 2, 256, 256), jnp.bfloat16),
            pltpu.SemaphoreType.DMA((GROUPS,)),
            pltpu.SemaphoreType.DMA((2, GROUPS)),
            pltpu.SemaphoreType.DMA((2, GROUPS)),
            pltpu.SemaphoreType.DMA((GROUPS,)),
            pltpu.SemaphoreType.DMA((2,)),
            pltpu.SemaphoreType.DMA((10,)),
        ],
        compiler_params=pltpu.CompilerParams(vmem_limit_bytes=44 * 2**20, collective_id=0, has_side_effects=True),
        cost_estimate=pl.CostEstimate(flops=10**10, bytes_accessed=16 * 2**20, transcendentals=0),
    )(voltages, order_table, pfb_taps)


def arrange_kernel(lag_table, near, mirror, far, visibility, far_visibility, sems):
    far_copy = pltpu.make_async_copy(far, far_visibility.at[:, 0], sems.at[0])
    far_copy.start()
    for slot in range(4):
        lag = lag_table[slot]

        @pl.when(lag == 0)
        def _(slot=slot):
            for out in range(8):
                pltpu.make_async_copy(mirror.at[out], visibility.at[out, 0, slot], sems.at[slot + 1]).start()

        @pl.when(lag > 0)
        def _(slot=slot, lag=lag):
            for out in range(8):
                pltpu.make_async_copy(near.at[out, pl.ds((lag - 1) * 2, 2)], visibility.at[out, 0, slot], sems.at[slot + 1]).start()

    for slot in range(4):
        pltpu.make_async_copy(mirror, visibility.at[:, 0, slot], sems.at[slot + 1]).wait()
    far_copy.wait()


def arrange(near, mirror, far, lag_table):
    return pl.pallas_call(
        arrange_kernel,
        out_shape=(
            jax.ShapeDtypeStruct((8, 1, 4, 2, 256, 256), jnp.bfloat16),
            jax.ShapeDtypeStruct((4, 1, 2, 256, 256), jnp.bfloat16),
        ),
        in_specs=[pl.BlockSpec(memory_space=pltpu.SMEM)] + [pl.BlockSpec(memory_space=pltpu.VMEM)] * 3,
        out_specs=(pl.BlockSpec(memory_space=pl.ANY), pl.BlockSpec(memory_space=pl.ANY)),
        scratch_shapes=[pltpu.SemaphoreType.DMA((5,))],
        compiler_params=pltpu.CompilerParams(vmem_limit_bytes=2**20),
    )(lag_table, near, mirror, far)


def per_device(voltages, pfb_taps, order_table, lag_table):
    near, mirror, far = make_tiles(voltages, pfb_taps, order_table)
    return arrange(near, mirror, far, lag_table)


def solution(mesh):
    placed = (P(None, ("freq", "blk"), None), P(), P("blk", None), P())
    return jax.shard_map(
        per_device,
        mesh=mesh,
        in_specs=placed,
        out_specs=(P("freq", "blk", None, None, None, None), P("freq", "blk", None, None, None)),
        check_vma=False,
    )
```
